32 devices in a mesh: lat: 4 (over z), lon: 8 (over y, x, core).
Axes of the slice: x: 2, y: 2, z: 4, core: 2. Of those that a mesh axis runs over, the one named last changes fastest.
Arguments:
- ice_state: float32 [5, 512, 2048], P(None, 'lat', 'lon'), may hold values from -6 to 6
- ocean_forcing: float32 [4, 512, 2048], P(None, 'lat', 'lon'), may hold values from -6 to 6
- ice_strength: float32 [512, 2048], P('lat', 'lon'), may hold values from 0.5 to 4
- ice_mask: int32 [512, 2048], P('lat', 'lon'), may hold values from 0 to 1, as said below
- yield_mask: int32 [6, 512, 2048], P(None, 'lat', 'lon'), may hold values 0 or 1
- ice_route: int32 [4, 4], replicated, may hold values from 0 to 3, each once within a row
Outputs:
- ocean_flux: float32 [2, 512, 2048], P(None, 'lat', 'lon')
- ice_blocks: float32 [16, 5, 32, 2048], P('lat', None, None, 'lon')
The draws below stay inside these ranges and needn't reach their ends.
Inputs may be any that keep to these rules, and one draw needn't show every extreme that they name: `ice_route`: each row is a permutation of 0 .. 3. `ice_mask`: ice is set block by block of 32 latitude rows: every block of the first and of the last latitude band may hold ice, and one or more blocks of every other band; in all other blocks it is 0.
All inputs are finite; a program needn't handle non-finite values. No bound on the sum of `yield_mask` on one device may be relied on, other than what follows from the above.
Results may differ from the reference program's by a relative error of at most 0.00011.
Values sent between devices are 32-bit elements; how exact they have to be, the bound alone decides.
No kernel may reach another device: no remote copies, remote signals or barrier semaphores. Data moves between devices by JAX's collectives and lax.ppermute only.
A program may use at most 128 MiB of HBM per device.

```python
import math
import jax
import jax.numpy as jnp

BY = 32
SUB = 6
CY = 128
NLAT = 512
NLON = 2048
N_LAT = 4


def draw_ice_mask(key, part):
    per_band = CY // BY
    bands = NLAT // CY
    block_count = NLAT // BY
    first, second, third = jax.random.split(key, 3)
    blocks = jnp.arange(block_count, dtype=jnp.int32)
    band_of = blocks // per_band
    within = blocks % per_band
    coins = jax.random.randint(first, (block_count,), 0, 4)
    chosen = jax.random.randint(second, (bands,), 0, per_band)
    icy_block = (band_of == 0) | (band_of == bands - 1) | (coins == 0) | (within == chosen[band_of])
    rows = jnp.arange(NLAT, dtype=jnp.int32) // BY
    icy_rows = icy_block[rows]
    cells = jax.random.randint(third, (NLAT, NLON), 0, 5)
    return jnp.where(icy_rows[:, None] & (cells > 0), 1, 0).astype(jnp.int32)


def touch_ends(values, rng, least, top_value):
    shape = values.shape
    place = [jax.random.randint(jax.random.fold_in(rng, axis), (), 0, shape[axis]) for axis in range(len(shape))]
    values = values.at[tuple(place)].set(least)
    longest = shape.index(max(shape))
    place[longest] = (place[longest] + 1) % shape[longest]
    return values.at[tuple(place)].set(top_value)


def levels(key, extent, shards, smallest, high):
    factor_of = 1.0
    for axis_at, shards_of in shards:
        draws = jax.random.uniform(jax.random.fold_in(jax.random.fold_in(key, 6), axis_at), (shards_of,), jnp.float32, smallest / len(shards), high / len(shards))
        factor_of = factor_of * jnp.repeat(jnp.exp(draws), extent[axis_at] // shards_of).reshape((-1,) + (1,) * (len(extent) - 1 - axis_at))
    return factor_of


def noise(rng, shape, spread, reach, cuts=(), kind=jnp.bfloat16):
    level = levels(rng, shape, cuts, -0.22, 0.18) if cuts else 1.0
    array = jax.random.normal(rng, shape, jnp.float32) * spread * level
    return jnp.minimum(jnp.maximum(array, -reach), reach).astype(kind)


def setup_inputs(seed: int = 0) -> dict:
    keys = jax.random.split(jax.random.key(seed), 7)
    ice_state = noise(keys[0], (5, NLAT, NLON), 1.0, 6.0, ((1, 4), (2, 8)), jnp.float32)
    ocean_forcing = noise(keys[1], (4, NLAT, NLON), 1.0, 6.0, ((1, 4), (2, 8)), jnp.float32)
    ice_strength = jnp.clip(jnp.exp(math.log(4.0) - 2.0794415 * jax.random.uniform(keys[2], (NLAT, NLON), jnp.float32) ** levels(keys[2], (NLAT, NLON), ((0, 4), (1, 8)), -0.2, 0.2)), 0.5, 4.0)
    ice_mask = draw_ice_mask(jax.random.fold_in(keys[6], 71), 0)
    yield_mask = touch_ends((jax.random.randint(keys[4], (SUB, NLAT, NLON), 0, 2) < 1).astype(jnp.int32), jax.random.fold_in(keys[4], 1), 0, 1)
    ice_route = jax.vmap(lambda own: jax.random.permutation(own, N_LAT))(jax.random.split(keys[5], N_LAT)).reshape((N_LAT, N_LAT)).astype(jnp.int32)
    return dict(ice_state=ice_state, ocean_forcing=ocean_forcing, ice_strength=ice_strength, ice_mask=ice_mask, yield_mask=yield_mask, ice_route=ice_route)


RELAX_RATE = 1.0
STEP_WEIGHT = 0.5
DRAG_COEF = 0.5
CORIOLIS = 0.3


def inner(field, depth):
    return field[..., depth:field.shape[-2] - depth, depth:field.shape[-1] - depth]


def subcycle(state, forcing, ice, regime):
    velo_x, velo_y = state[0], state[1]
    stretch_x = (velo_x[1:-1, 2:] - velo_x[1:-1, :-2]) * 0.5
    stretch_y = (velo_y[2:, 1:-1] - velo_y[:-2, 1:-1]) * 0.5
    cross_x = (velo_x[2:, 1:-1] - velo_x[:-2, 1:-1]) * 0.5
    cross_y = (velo_y[1:-1, 2:] - velo_y[1:-1, :-2]) * 0.5
    strength = inner(forcing[4], 1)
    ice_one = inner(ice, 1)
    viscous = strength * (1.5 - inner(regime, 1))
    keep = 1.0 / (1.0 + RELAX_RATE)
    new_sum = ice_one * (inner(state[2], 1) + RELAX_RATE * (viscous * (stretch_x + stretch_y) - 0.5 * strength)) * keep
    new_diff = ice_one * (inner(state[3], 1) + RELAX_RATE * 0.5 * viscous * (stretch_x - stretch_y)) * keep
    new_shear = ice_one * (inner(state[4], 1) + RELAX_RATE * 0.25 * viscous * (cross_x + cross_y)) * keep
    normal_x = new_sum + new_diff
    normal_y = new_sum - new_diff
    force_x = (normal_x[1:-1, 2:] - normal_x[1:-1, :-2]) * 0.25 + (new_shear[2:, 1:-1] - new_shear[:-2, 1:-1]) * 0.5
    force_y = (normal_y[2:, 1:-1] - normal_y[:-2, 1:-1]) * 0.25 + (new_shear[1:-1, 2:] - new_shear[1:-1, :-2]) * 0.5
    ice_two = inner(ice, 2)
    old_x = inner(velo_x, 2)
    old_y = inner(velo_y, 2)
    damp = 1.0 / (1.0 + STEP_WEIGHT * DRAG_COEF)
    next_x = ice_two * (old_x + STEP_WEIGHT * (force_x + inner(forcing[0], 2) + DRAG_COEF * inner(forcing[2], 2) + CORIOLIS * old_y)) * damp
    next_y = ice_two * (old_y + STEP_WEIGHT * (force_y + inner(forcing[1], 2) + DRAG_COEF * inner(forcing[3], 2) - CORIOLIS * old_x)) * damp
    return jnp.stack([next_x, next_y, inner(new_sum, 1), inner(new_diff, 1), inner(new_shear, 1)])


def evolve(state, forcing, ice, regimes):
    for level in range(regimes.shape[0]):
        trim = 2 * level
        state = subcycle(state, inner(forcing, trim), inner(ice, trim), inner(regimes[level], trim))
    return state


def reference(ice_state, ocean_forcing, ice_strength, ice_mask, yield_mask, ice_route):
    depth = 2 * SUB

    def widen(field):
        field = jnp.concatenate([field[..., -depth:], field, field[..., :depth]], axis=-1)
        widths = [(0, 0)] * (field.ndim - 2) + [(depth, depth), (0, 0)]
        return jnp.pad(field, widths)

    forcing = jnp.concatenate([ocean_forcing, ice_strength[None]], axis=0)
    ice_f = ice_mask.astype(jnp.float32)
    final = evolve(widen(ice_state), widen(forcing), widen(ice_f), widen(yield_mask.astype(jnp.float32)))
    ocean_flux = DRAG_COEF * ice_f[None] * (final[:2] - ocean_forcing[2:4])
    blocks = final.reshape(5, N_LAT, N_LAT, BY, NLON)
    lanes = jnp.arange(N_LAT, dtype=jnp.int32)
    match = (ice_route[:, :, None] == lanes[None, None, :]).astype(jnp.int32)
    inverse = jnp.sum(match * lanes[None, :, None], axis=1)
    source = jnp.broadcast_to(lanes[None, :], (N_LAT, N_LAT))
    picked = blocks[:, source, inverse.T]
    ice_blocks = picked.transpose(1, 2, 0, 3, 4).reshape(N_LAT * N_LAT, 5, BY, NLON)
    return ocean_flux, ice_blocks
```

```python
import functools
import jax
import jax.numpy as jnp
from jax import lax
from jax.experimental import pallas as pl
from jax.experimental.pallas import tpu as pltpu
from jax.sharding import PartitionSpec as P

DRAG = 0.5
SPIN = 0.15
DAMP = 0.8
LANES = 128
PAD = 24
FIELDS = 9
VMEM = pltpu.VMEM


def lane_index(rows):
    return lax.broadcasted_iota(jnp.int32, (rows, LANES), 1)


def raw_fields(state, forcing, strength, ice, regimes, at):
    count = regimes.shape[0]
    s_one, s_two = (state[(2, *at)], state[(3, *at)])
    code = ice[at]
    for level in range(count):
        code = code + regimes[(level, *at)] * (2 << level)
    return [
        state[(0, *at)],
        state[(1, *at)],
        s_one + s_two,
        s_one - s_two,
        2.0 * state[(4, *at)],
        forcing[(0, *at)] + DRAG * forcing[(2, *at)],
        forcing[(1, *at)] + DRAG * forcing[(3, *at)],
        strength[at],
        code.astype(jnp.float32),
    ]


def pack_kernel(depth, state, forcing, strength, ice, regimes, to_west, to_east, to_south, to_north):
    rows, columns = strength.shape
    step = 32
    lane = lane_index(step)
    for top in range(0, rows, step):
        span = pl.ds(top, step)
        first = raw_fields(state, forcing, strength, ice, regimes, (span, pl.ds(0, LANES)))
        last = raw_fields(state, forcing, strength, ice, regimes, (span, pl.ds(columns - LANES, LANES)))
        west = first[0]
        east = pltpu.roll(last[0], depth, 1)
        for field in range(1, FIELDS):
            slot = lane >= depth * field
            west = jnp.where(slot, pltpu.roll(first[field], depth * field, 1), west)
            east = jnp.where(slot, pltpu.roll(last[field], depth * (field + 1), 1), east)
        to_west[span, :] = west
        to_east[span, :] = east
    for target, top in ((to_south, 0), (to_north, rows - 16)):
        skip = 0 if top == 0 else 16 - depth
        for column in range(0, columns, LANES):
            at = (pl.ds(top, 16), pl.ds(column, LANES))
            for field, value in enumerate(raw_fields(state, forcing, strength, ice, regimes, at)):
                target[pl.ds(depth * field, depth), pl.ds(column, LANES)] = value[skip : skip + depth]


def evolve_kernel(
    depth, blocks, slots_ref, state, forcing, strength, ice, regimes,
    from_west, from_east, from_south, from_north, flux, outgoing, live, coef, code_ref,
):
    rows, columns = strength.shape
    count = regimes.shape[0]
    tiles = columns // LANES
    halo = tiles
    high = rows + 2 * PAD

    def place(tile, top, size, fields):
        u, v, a, b, t, fx, fy, strong, code = fields
        span = pl.ds(top, size)
        code = code.astype(jnp.int32)
        icy = (code & 1).astype(jnp.float32)
        live[0, tile, span, :] = u
        live[1, tile, span, :] = v
        live[2, tile, span, :] = icy * a
        live[3, tile, span, :] = icy * b
        live[4, tile, span, :] = icy * t
        coef[0, tile, span, :] = 0.25 * icy * strong
        coef[1, tile, span, :] = DAMP * icy
        coef[2, tile, span, :] = (0.5 * DAMP) * icy * fx
        coef[3, tile, span, :] = (0.5 * DAMP) * icy * fy
        code_ref[tile, span, :] = code

    def rim(west, east, size):
        lane = lane_index(size)
        fields = []
        for field in range(FIELDS):
            right = pltpu.roll(east, (LANES - depth * field) % LANES, 1)
            left = pltpu.roll(west, (2 * LANES - depth * (field + 1)) % LANES, 1)
            fields.append(jnp.where(lane < depth, right, jnp.where(lane >= LANES - depth, left, 0.0)))
        return fields

    zero = jnp.zeros((PAD, LANES), jnp.float32)
    for tile in range(tiles + 1):
        for top in (0, rows + PAD):
            span = pl.ds(top, PAD)
            for field in range(5):
                live[field, tile, span, :] = zero
            for field in range(4):
                coef[field, tile, span, :] = zero
            code_ref[tile, span, :] = zero.astype(jnp.int32)
    for tile in range(tiles):
        for top in range(0, rows, 32):
            at = (pl.ds(top, 32), pl.ds(tile * LANES, LANES))
            place(tile, PAD + top, 32, raw_fields(state, forcing, strength, ice, regimes, at))
    for top in range(0, rows, 32):
        span = pl.ds(top, 32)
        place(halo, PAD + top, 32, rim(from_west[span, :], from_east[span, :], 32))
    for source, top in ((from_north, PAD - depth), (from_south, PAD + rows)):
        for tile in range(tiles):
            columns_at = pl.ds(tile * LANES, LANES)
            place(tile, top, depth, [source[pl.ds(depth * f, depth), columns_at] for f in range(FIELDS)])
        corner = pl.ds(depth * FIELDS, depth)
        place(halo, top, depth, rim(source[corner, pl.ds(0, LANES)], source[corner, pl.ds(LANES, LANES)], depth))

    size = 8
    lane = lane_index(size)
    first_lane = lane == 0
    last_lane = lane == LANES - 1

    def across(parts):
        back = [pltpu.roll(part, 1, 1) for part in parts]
        ahead = [pltpu.roll(part, LANES - 1, 1) for part in parts]
        wide = len(parts)
        return [
            jnp.where(last_lane, ahead[(i + 1) % wide], ahead[i])
            - jnp.where(first_lane, back[i - 1], back[i])
            for i in range(wide)
        ]

    def row(field, tile, top):
        return live[field, tile, pl.ds(top, size), :]

    def down(field, tile, top):
        return row(field, tile, top + 1) - row(field, tile, top - 1)

    def sweep(level, carry):
        bit = lax.shift_left(2, level)
        every = range(tiles + 1)
        for top in range(8, high - 8, size):
            span = pl.ds(top, size)
            du_dx = across([row(0, i, top) for i in every])
            dv_dx = across([row(1, i, top) for i in every])
            for i in every:
                dv_dy = down(1, i, top)
                du_dy = down(0, i, top)
                base = coef[0, i, span, :]
                weak = (code_ref[i, span, :] & bit) != 0
                scale = base * jnp.where(weak, 0.5, 1.5)
                half = 0.5 * (du_dx[i] + dv_dy)
                live[2, i, span, :] = 0.5 * row(2, i, top) + (scale * (du_dx[i] + half) - base)
                live[3, i, span, :] = 0.5 * row(3, i, top) + (scale * (dv_dy + half) - base)
                live[4, i, span, :] = 0.5 * (row(4, i, top) + scale * (du_dy + dv_dx[i]))
        for top in range(8, high - 8, size):
            span = pl.ds(top, size)
            da_dx = across([row(2, i, top) for i in every])
            dt_dx = across([row(4, i, top) for i in every])
            for i in every:
                u, v = (row(0, i, top), row(1, i, top))
                damp = coef[1, i, span, :]
                pull_x = 0.125 * (da_dx[i] + down(4, i, top))
                pull_y = 0.125 * (down(3, i, top) + dt_dx[i])
                live[0, i, span, :] = damp * (u + SPIN * v + pull_x) + coef[2, i, span, :]
                live[1, i, span, :] = damp * (v - SPIN * u + pull_y) + coef[3, i, span, :]
        return carry

    lax.fori_loop(0, count, sweep, 0)

    block_rows = rows // blocks
    for block in range(blocks):
        slot = slots_ref[block]
        for tile in range(tiles):
            column = pl.ds(tile * LANES, LANES)
            span = pl.ds(PAD + block * block_rows, block_rows)
            here = pl.ds(block * block_rows, block_rows)
            u, v, a, b, t = (live[field, tile, span, :] for field in range(5))
            icy = DRAG * ice[here, column].astype(jnp.float32)
            flux[0, here, column] = icy * (u - forcing[2, here, column])
            flux[1, here, column] = icy * (v - forcing[3, here, column])
            outgoing[slot, 0, :, column] = u
            outgoing[slot, 1, :, column] = v
            outgoing[slot, 2, :, column] = 0.5 * (a + b)
            outgoing[slot, 3, :, column] = 0.5 * (a - b)
            outgoing[slot, 4, :, column] = 0.5 * t


def whole():
    return pl.BlockSpec(memory_space=VMEM)


def per_device(ice_state, ocean_forcing, ice_strength, ice_mask, yield_mask, ice_route):
    f32 = jnp.float32
    depth = 2 * yield_mask.shape[0]
    rows, columns = ice_strength.shape
    lats, lons = (lax.axis_size("lat"), lax.axis_size("lon"))
    raw = (ice_state, ocean_forcing, ice_strength, ice_mask, yield_mask)
    shape = jax.ShapeDtypeStruct
    to_west, to_east, to_south, to_north = pl.pallas_call(
        functools.partial(pack_kernel, depth),
        out_shape=[shape((rows, LANES), f32)] * 2 + [shape((depth * FIELDS, columns), f32)] * 2,
        in_specs=[whole()] * 5,
        out_specs=[whole()] * 4,
        compiler_params=pltpu.CompilerParams(vmem_limit_bytes=32 << 20),
        name="pack",
    )(*raw)
    from_west = lax.ppermute(to_east, "lon", [(i, (i + 1) % lons) for i in range(lons)])
    from_east = lax.ppermute(to_west, "lon", [((i + 1) % lons, i) for i in range(lons)])

    def with_corner(rim, top):
        span = slice(top, top + depth)
        corner = [from_west[span], from_east[span]]
        if columns > 2 * LANES:
            corner.append(jnp.zeros((depth, columns - 2 * LANES), f32))
        return jnp.concatenate([rim, jnp.concatenate(corner, axis=1)], axis=0)

    from_south = lax.ppermute(with_corner(to_south, 0), "lat", [(i + 1, i) for i in range(lats - 1)])
    from_north = lax.ppermute(with_corner(to_north, rows - depth), "lat", [(i, i + 1) for i in range(lats - 1)])
    slots = lax.dynamic_index_in_dim(ice_route, lax.axis_index("lat"), keepdims=False)
    high = rows + 2 * PAD
    tiles = columns // LANES + 1
    flux, outgoing = pl.pallas_call(
        functools.partial(evolve_kernel, depth, lats),
        out_shape=[shape((2, rows, columns), f32), shape((lats, 5, rows // lats, columns), f32)],
        in_specs=[pl.BlockSpec(memory_space=pltpu.SMEM)] + [whole()] * 9,
        out_specs=[whole()] * 2,
        scratch_shapes=[
            VMEM((5, tiles, high, LANES), f32),
            VMEM((4, tiles, high, LANES), f32),
            VMEM((tiles, high, LANES), jnp.int32),
        ],
        compiler_params=pltpu.CompilerParams(vmem_limit_bytes=32 << 20),
        name="evolve",
    )(slots, *raw, from_west, from_east, from_south, from_north)
    return flux, lax.all_to_all(outgoing, "lat", split_axis=0, concat_axis=0, tiled=True)


def solution(mesh):
    return jax.shard_map(
        per_device,
        mesh=mesh,
        in_specs=(
            P(None, "lat", "lon"),
            P(None, "lat", "lon"),
            P("lat", "lon"),
            P("lat", "lon"),
            P(None, "lat", "lon"),
            P(),
        ),
        out_specs=(P(None, "lat", "lon"), P("lat", None, None, "lon")),
        check_vma=False,
    )
```

```python
import functools
import jax
import jax.numpy as jnp
from jax import lax
from jax.experimental import pallas as pl
from jax.experimental.pallas import tpu as pltpu
from jax.sharding import PartitionSpec as P

DRAG = 0.5
SPIN = 0.15
DAMP = 0.8
LANES = 128
PAD = 24
FIELDS = 9
VMEM = pltpu.VMEM
HBM = pltpu.HBM


def lane_index(rows):
    return lax.broadcasted_iota(jnp.int32, (rows, LANES), 1)


def raw_fields(state, forcing, strength, ice, regimes, at):
    count = regimes.shape[0]
    s_one, s_two = (state[(2, *at)], state[(3, *at)])
    code = ice[at]
    for level in range(count):
        code = code + regimes[(level, *at)] * (2 << level)
    return [
        state[(0, *at)],
        state[(1, *at)],
        s_one + s_two,
        s_one - s_two,
        2.0 * state[(4, *at)],
        forcing[(0, *at)] + DRAG * forcing[(2, *at)],
        forcing[(1, *at)] + DRAG * forcing[(3, *at)],
        strength[at],
        code.astype(jnp.float32),
    ]


def both_axes():
    return (lax.axis_index("lat"), lax.axis_index("lon"))


def roll_to(value, shift):
    return value if shift % LANES == 0 else pltpu.roll(value, shift % LANES, 1)


def slotted(values, depth, start):
    lane = lane_index(values[0].shape[0])
    packed = roll_to(values[0], -start)
    for field in range(1, FIELDS):
        packed = jnp.where(lane >= depth * field, roll_to(values[field], depth * field - start), packed)
    return packed


def unslotted(west, east, depth):
    lane = lane_index(west.shape[0])
    fields = []
    for field in range(FIELDS):
        right = roll_to(east, -depth * field)
        left = roll_to(west, -depth * (field + 1))
        fields.append(jnp.where(lane < depth, right, jnp.where(lane >= LANES - depth, left, 0.0)))
    return fields


def pack_kernel(depth, *refs):
    sources, (lon_a, lon_b, lat_a, lat_b), raw, sem = refs[:5], refs[5:9], refs[9:14], refs[14]
    copies = [pltpu.make_async_copy(a, b, sem.at[i]) for i, (a, b) in enumerate(zip(sources, raw))]
    for copy in copies:
        copy.start()
    for copy in copies:
        copy.wait()
    rows, columns = raw[2].shape
    lat, lon = both_axes()
    lat_even = lax.rem(lat, 2) == 0
    lon_even = lax.rem(lon, 2) == 0
    step = 32
    for top in range(0, rows, step):
        span = pl.ds(top, step)
        first = slotted(raw_fields(*raw, (span, pl.ds(0, LANES))), depth, 0)
        last = slotted(raw_fields(*raw, (span, pl.ds(columns - LANES, LANES))), depth, LANES - depth)
        lon_a[span, :] = jnp.where(lon_even, last, first)
        lon_b[span, :] = jnp.where(lon_even, first, last)
    for column in range(0, columns, LANES):
        here = pl.ds(column, LANES)
        first = raw_fields(*raw, (pl.ds(0, 16), here))
        last = raw_fields(*raw, (pl.ds(rows - 16, 16), here))
        for field in range(FIELDS):
            span = pl.ds(depth * field, depth)
            one, two = (first[field][:depth], last[field][16 - depth :])
            lat_a[span, here] = jnp.where(lat_even, two, one)
            lat_b[span, here] = jnp.where(lat_even, one, two)


def corner_kernel(depth, lat_a, lat_b, out_a, out_b):
    columns = lat_a.shape[1]
    lon_even = lax.rem(lax.axis_index("lon"), 2) == 0
    for source, top in ((lat_a, 0), (lat_b, 16)):
        def fields(column):
            return [source[pl.ds(depth * f, depth), pl.ds(column, LANES)] for f in range(FIELDS)]

        first = slotted(fields(0), depth, 0)
        last = slotted(fields(columns - LANES), depth, LANES - depth)
        out_a[pl.ds(top, depth), :] = jnp.where(lon_even, last, first)
        out_b[pl.ds(top, depth), :] = jnp.where(lon_even, first, last)


def place(live, coef, code_ref, tile, top, size, fields):
    u, v, a, b, t, fx, fy, strong, code = fields
    span = pl.ds(top, size)
    code = code.astype(jnp.int32)
    icy = (code & 1).astype(jnp.float32)
    live[0, tile, span, :] = u
    live[1, tile, span, :] = v
    live[2, tile, span, :] = icy * a
    live[3, tile, span, :] = icy * b
    live[4, tile, span, :] = icy * t
    coef[0, tile, span, :] = 0.25 * icy * strong
    coef[1, tile, span, :] = DAMP * icy
    coef[2, tile, span, :] = (0.5 * DAMP) * icy * fx
    coef[3, tile, span, :] = (0.5 * DAMP) * icy * fy
    code_ref[tile, span, :] = code


def prepare_kernel(state, forcing, strength, ice, regimes, live, coef, code_ref):
    rows, columns = strength.shape
    tiles = columns // LANES
    zero = jnp.zeros((PAD, LANES), jnp.float32)
    for tile in range(tiles + 1):
        for top in (0, rows + PAD):
            span = pl.ds(top, PAD)
            for field in range(5):
                live[field, tile, span, :] = zero
            for field in range(4):
                coef[field, tile, span, :] = zero
            code_ref[tile, span, :] = zero.astype(jnp.int32)
    for tile in range(tiles):
        for top in range(0, rows, 32):
            at = (pl.ds(top, 32), pl.ds(tile * LANES, LANES))
            fields = raw_fields(state, forcing, strength, ice, regimes, at)
            place(live, coef, code_ref, tile, PAD + top, 32, fields)


def evolve_kernel(
    depth, count, blocks, route, forcing, ice, lon_a, lon_b, lat_a, lat_b, corner_a, corner_b,
    live_in, coef_in, code_in, live, coef, code_ref, flux, *outgoing,
):
    rows, columns = ice.shape
    tiles = columns // LANES
    halo = tiles
    high = rows + 2 * PAD
    lat, lon = both_axes()
    lat_even = lax.rem(lat, 2) == 0
    lon_even = lax.rem(lon, 2) == 0

    def rim(a, b):
        return unslotted(jnp.where(lon_even, b, a), jnp.where(lon_even, a, b), depth)

    for top in range(0, rows, 32):
        span = pl.ds(top, 32)
        place(live, coef, code_ref, halo, PAD + top, 32, rim(lon_a[span, :], lon_b[span, :]))
    south = jnp.where(lat == blocks - 1, 0.0, 1.0)
    north = jnp.where(lat == 0, 0.0, 1.0)
    for top, other in ((PAD + rows, False), (PAD - depth, True)):
        keep = north if other else south

        def chosen(a, b):
            return keep * (jnp.where(lat_even, b, a) if other else jnp.where(lat_even, a, b))

        for tile in range(tiles):
            here = pl.ds(tile * LANES, LANES)
            spans = [pl.ds(depth * f, depth) for f in range(FIELDS)]
            place(live, coef, code_ref, tile, top, depth, [chosen(lat_a[s, here], lat_b[s, here]) for s in spans])
        one, two = (pl.ds(0, depth), pl.ds(16, depth))
        corners = rim(chosen(corner_a[one, :], corner_a[two, :]), chosen(corner_b[one, :], corner_b[two, :]))
        place(live, coef, code_ref, halo, top, depth, corners)

    size = 8
    lane = lane_index(size)
    first_lane = lane == 0
    last_lane = lane == LANES - 1
    every = range(tiles + 1)

    def across(parts):
        back = [pltpu.roll(part, 1, 1) for part in parts]
        ahead = [pltpu.roll(part, LANES - 1, 1) for part in parts]
        wide = len(parts)
        return [
            jnp.where(last_lane, ahead[(i + 1) % wide], ahead[i])
            - jnp.where(first_lane, back[i - 1], back[i])
            for i in range(wide)
        ]

    def row(field, tile, top):
        return live[field, tile, pl.ds(top, size), :]

    def down(field, tile, top):
        return row(field, tile, top + 1) - row(field, tile, top - 1)

    def reach(cells):
        return range((PAD - cells) // 8 * 8, PAD + rows + cells, size)

    for level in range(count):
        left = depth - 2 * level
        for top in reach(left - 1):
            span = pl.ds(top, size)
            du_dx = across([row(0, i, top) for i in every])
            dv_dx = across([row(1, i, top) for i in every])
            for i in every:
                dv_dy = down(1, i, top)
                du_dy = down(0, i, top)
                base = coef[0, i, span, :]
                weak = (code_ref[i, span, :] & (2 << level)) != 0
                scale = base * jnp.where(weak, 0.5, 1.5)
                half = 0.5 * (du_dx[i] + dv_dy)
                live[2, i, span, :] = 0.5 * row(2, i, top) + (scale * (du_dx[i] + half) - base)
                live[3, i, span, :] = 0.5 * row(3, i, top) + (scale * (dv_dy + half) - base)
                live[4, i, span, :] = 0.5 * (row(4, i, top) + scale * (du_dy + dv_dx[i]))
        for top in reach(left - 2):
            span = pl.ds(top, size)
            da_dx = across([row(2, i, top) for i in every])
            dt_dx = across([row(4, i, top) for i in every])
            for i in every:
                u, v = (row(0, i, top), row(1, i, top))
                damp = coef[1, i, span, :]
                pull_x = 0.125 * (da_dx[i] + down(4, i, top))
                pull_y = 0.125 * (down(3, i, top) + dt_dx[i])
                live[0, i, span, :] = damp * (u + SPIN * v + pull_x) + coef[2, i, span, :]
                live[1, i, span, :] = damp * (v - SPIN * u + pull_y) + coef[3, i, span, :]

    tall = rows // blocks
    for hop, target in enumerate(outgoing):
        to = lat ^ hop
        block = sum(jnp.where(route[lat, j] == to, j, 0) for j in range(blocks))
        span = pl.ds(pl.multiple_of(PAD + block * tall, 8), tall)
        for tile in range(tiles):
            column = pl.ds(tile * LANES, LANES)
            u, v, a, b, t = (live[field, tile, span, :] for field in range(5))
            target[0, :, column] = u
            target[1, :, column] = v
            target[2, :, column] = 0.5 * (a + b)
            target[3, :, column] = 0.5 * (a - b)
            target[4, :, column] = 0.5 * t
    for tile in range(tiles):
        for top in range(0, rows, 32):
            at = (pl.ds(top, 32), pl.ds(tile * LANES, LANES))
            span = pl.ds(PAD + top, 32)
            icy = DRAG * ice[at].astype(jnp.float32)
            flux[(0, *at)] = icy * (live[0, tile, span, :] - forcing[(2, *at)])
            flux[(1, *at)] = icy * (live[1, tile, span, :] - forcing[(3, *at)])


def gather_kernel(*refs):
    parts, out, sem = refs[:-2], refs[-2], refs[-1]
    lat = lax.axis_index("lat")
    copies = [pltpu.make_async_copy(part, out.at[lat ^ hop], sem.at[hop]) for hop, part in enumerate(parts)]
    for copy in copies:
        copy.start()
    for copy in copies:
        copy.wait()


def spec(space=VMEM):
    return pl.BlockSpec(memory_space=space)


def params():
    return pltpu.CompilerParams(vmem_limit_bytes=16 << 20)


def cost(flops, data):
    return pl.CostEstimate(flops=flops, bytes_accessed=data, transcendentals=0)


def lon_swaps(a, b, lons):
    near = [(i, i ^ 1) for i in range(lons)]
    far = [(i, (i + 1 if i % 2 else i - 1) % lons) for i in range(lons)]
    return lax.ppermute(a, "lon", near), lax.ppermute(b, "lon", far)


def lat_swaps(a, b, lats, lons):
    near = [(i, i ^ 1) for i in range(lats)]
    far = []
    for i in range(lats):
        for j in range(lons):
            if i in (0, lats - 1):
                far.append((i * lons + j, i * lons + (j ^ 1)))
            else:
                far.append((i * lons + j, (i + 1 if i % 2 else i - 1) * lons + j))
    return lax.ppermute(a, "lat", near), lax.ppermute(b, ("lat", "lon"), far)


def per_device(ice_state, ocean_forcing, ice_strength, ice_mask, yield_mask, ice_route):
    f32 = jnp.float32
    count = yield_mask.shape[0]
    depth = 2 * count
    rows, columns = ice_strength.shape
    lats, lons = (lax.axis_size("lat"), lax.axis_size("lon"))
    inputs = (ice_state, ocean_forcing, ice_strength, ice_mask, yield_mask)
    shape = jax.ShapeDtypeStruct
    lon_rim = shape((rows, LANES), f32)
    lat_rim = shape((depth * FIELDS, columns), f32)
    corner = shape((32, LANES), f32)
    high = rows + 2 * PAD
    tiles = columns // LANES + 1
    fields = [
        shape((5, tiles, high, LANES), f32),
        shape((4, tiles, high, LANES), f32),
        shape((tiles, high, LANES), jnp.int32),
    ]
    lon_a, lon_b, lat_a, lat_b, *raw = pl.pallas_call(
        functools.partial(pack_kernel, depth),
        out_shape=[lon_rim] * 2 + [lat_rim] * 2 + [shape(x.shape, x.dtype) for x in inputs],
        in_specs=[spec(HBM)] * 5,
        out_specs=[spec()] * 9,
        scratch_shapes=[pltpu.SemaphoreType.DMA((5,))],
        compiler_params=params(),
        name="pack",
    )(*inputs)
    lat_a, lat_b = lat_swaps(lat_a, lat_b, lats, lons)
    lon_a, lon_b = lon_swaps(lon_a, lon_b, lons)
    prepared = pl.pallas_call(
        prepare_kernel,
        out_shape=fields,
        in_specs=[spec()] * 5,
        out_specs=[spec()] * 3,
        compiler_params=params(),
        cost_estimate=cost(40 * rows * columns, 100 * rows * columns),
        name="prepare",
    )(*raw)
    corner_a, corner_b = pl.pallas_call(
        functools.partial(corner_kernel, depth),
        out_shape=[corner] * 2,
        in_specs=[spec()] * 2,
        out_specs=[spec()] * 2,
        compiler_params=params(),
        name="corner",
    )(lat_a, lat_b)
    corner_a, corner_b = lon_swaps(corner_a, corner_b, lons)
    block = shape((5, rows // lats, columns), f32)
    _, _, _, flux, *outgoing = pl.pallas_call(
        functools.partial(evolve_kernel, depth, count, lats),
        out_shape=fields + [shape((2, rows, columns), f32)] + [block] * lats,
        in_specs=[spec(pltpu.SMEM)] + [spec()] * 11,
        out_specs=[spec()] * (4 + lats),
        input_output_aliases={9: 0, 10: 1, 11: 2},
        compiler_params=params(),
        name="evolve",
    )(ice_route, raw[1], raw[3], lon_a, lon_b, lat_a, lat_b, corner_a, corner_b, *prepared)
    parts = [outgoing[0]] + [None] * (lats - 1)
    for hop in range(lats - 1, 0, -1):
        parts[hop] = lax.ppermute(outgoing[hop], "lat", [(i, i ^ hop) for i in range(lats)])
    blocks = pl.pallas_call(
        gather_kernel,
        out_shape=shape((lats, *block.shape), f32),
        in_specs=[spec()] * lats,
        out_specs=spec(HBM),
        scratch_shapes=[pltpu.SemaphoreType.DMA((lats,))],
        compiler_params=params(),
        name="gather",
    )(*parts)
    return flux, blocks


def solution(mesh):
    return jax.shard_map(
        per_device,
        mesh=mesh,
        in_specs=(
            P(None, "lat", "lon"),
            P(None, "lat", "lon"),
            P("lat", "lon"),
            P("lat", "lon"),
            P(None, "lat", "lon"),
            P(),
        ),
        out_specs=(P(None, "lat", "lon"), P("lat", None, None, "lon")),
        check_vma=False,
    )
```

```python
import functools
import jax
import jax.numpy as jnp
from jax import lax
from jax.experimental import pallas as pl
from jax.experimental.pallas import tpu as pltpu
from jax.sharding import PartitionSpec as P

DRAG = 0.5
SPIN = 0.15
DAMP = 0.8
LANES = 128
PAD = 8
BAND = 64
EDGE = 24
HALF = 16
FIELDS = 9
VMEM = pltpu.VMEM
HBM = pltpu.HBM


def lane_index(rows):
    return lax.broadcasted_iota(jnp.int32, (rows, LANES), 1)


def raw_fields(state, forcing, strength, ice, regimes, at):
    count = regimes.shape[0]
    s_one, s_two = (state[(2, *at)], state[(3, *at)])
    code = ice[at]
    for level in range(count):
        code = code + regimes[(level, *at)] * (2 << level)
    return [
        state[(0, *at)],
        state[(1, *at)],
        s_one + s_two,
        s_one - s_two,
        2.0 * state[(4, *at)],
        forcing[(0, *at)] + DRAG * forcing[(2, *at)],
        forcing[(1, *at)] + DRAG * forcing[(3, *at)],
        strength[at],
        code.astype(jnp.float32),
    ]


def both_axes():
    return (lax.axis_index("lat"), lax.axis_index("lon"))


def roll_to(value, shift):
    return value if shift % LANES == 0 else pltpu.roll(value, shift % LANES, 1)


def slotted(values, depth, start):
    lane = lane_index(values[0].shape[0])
    packed = roll_to(values[0], -start)
    for field in range(1, FIELDS):
        packed = jnp.where(lane >= depth * field, roll_to(values[field], depth * field - start), packed)
    return packed


def unslotted(west, east, depth):
    lane = lane_index(west.shape[0])
    fields = []
    for field in range(FIELDS):
        right = roll_to(east, -depth * field)
        left = roll_to(west, -depth * (field + 1))
        fields.append(jnp.where(lane < depth, right, jnp.where(lane >= LANES - depth, left, 0.0)))
    return fields


def pack_kernel(depth, *refs):
    sources, (lon_a, lon_b, lat_a, lat_b), raw, sem = refs[:6], refs[6:10], refs[10:16], refs[16]
    copies = [pltpu.make_async_copy(a, b, sem.at[i]) for i, (a, b) in enumerate(zip(sources, raw))]
    raw = raw[1:]
    for copy in copies:
        copy.start()
    for copy in copies:
        copy.wait()
    rows, columns = raw[2].shape
    lat, lon = both_axes()
    lat_even = lax.rem(lat, 2) == 0
    lon_even = lax.rem(lon, 2) == 0
    step = 32
    for top in range(0, rows, step):
        span = pl.ds(top, step)
        first = slotted(raw_fields(*raw, (span, pl.ds(0, LANES))), depth, 0)
        last = slotted(raw_fields(*raw, (span, pl.ds(columns - LANES, LANES))), depth, LANES - depth)
        lon_a[span, :] = jnp.where(lon_even, last, first)
        lon_b[span, :] = jnp.where(lon_even, first, last)
    for column in range(0, columns, LANES):
        here = pl.ds(column, LANES)
        first = raw_fields(*raw, (pl.ds(0, 16), here))
        last = raw_fields(*raw, (pl.ds(rows - 16, 16), here))
        for field in range(FIELDS):
            span = pl.ds(depth * field, depth)
            one, two = (first[field][:depth], last[field][16 - depth :])
            lat_a[span, here] = jnp.where(lat_even, two, one)
            lat_b[span, here] = jnp.where(lat_even, one, two)


def corner_kernel(depth, lon_a, lon_b, lat_a, lat_b, after, out_a, out_b):
    rows = lon_a.shape[0]
    lat_even = lax.rem(lax.axis_index("lat"), 2) == 0
    span = pl.ds(depth * FIELDS, depth)
    for source, column in ((lon_a, 0), (lon_b, LANES)):
        first = source[pl.ds(0, 16), :][:depth]
        last = source[pl.ds(rows - 16, 16), :][16 - depth :]
        out_a[span, pl.ds(column, LANES)] = jnp.where(lat_even, last, first)
        out_b[span, pl.ds(column, LANES)] = jnp.where(lat_even, first, last)


def place(live, coef, code_ref, tile, top, size, fields):
    u, v, a, b, t, fx, fy, strong, code = fields
    span = pl.ds(top, size)
    code = code.astype(jnp.int32)
    icy = (code & 1).astype(jnp.float32)
    live[0, tile, span, :] = u
    live[1, tile, span, :] = v
    live[2, tile, span, :] = icy * a
    live[3, tile, span, :] = icy * b
    live[4, tile, span, :] = icy * t
    coef[0, tile, span, :] = 0.25 * icy * strong
    coef[1, tile, span, :] = DAMP * icy
    coef[2, tile, span, :] = (0.5 * DAMP) * icy * fx
    coef[3, tile, span, :] = (0.5 * DAMP) * icy * fy
    code_ref[tile, span, :] = code


def prepare_kernel(route, state, forcing, strength, ice, regimes, *refs):
    inner, band, table = refs[:3], refs[3:6], refs[6]
    lat = lax.axis_index("lat")
    line, lane = (lax.broadcasted_iota(jnp.int32, table.shape, axis) for axis in range(2))
    found = jnp.zeros(table.shape, jnp.int32)
    for hop in range(route.shape[0]):
        other = lat ^ hop
        for index, block in enumerate((block_for(route, lat, other), block_for(route, other, lat))):
            found = jnp.where((line == index) & (lane == hop), block, found)
    table[...] = found
    rows, columns = strength.shape
    tiles = columns // LANES

    def clear(refs, tile, top, size):
        span = pl.ds(top, size)
        zero = jnp.zeros((size, LANES), jnp.float32)
        for ref in refs[:2]:
            for field in range(ref.shape[0]):
                ref[field, tile, span, :] = zero
        refs[2][tile, span, :] = zero.astype(jnp.int32)

    for tile in range(tiles):
        clear(inner, tile, 0, PAD)
        clear(inner, tile, PAD + rows, PAD)
    for tile in range(tiles + 1):
        clear(band, tile, 0, EDGE)
        clear(band, tile, EDGE + 32, BAND - EDGE - 32)
        clear(band, tiles + 1 + tile, 0, 8)
        clear(band, tiles + 1 + tile, 40, BAND - 40)
    for tile in range(tiles):
        for top in range(0, rows, 32):
            at = (pl.ds(top, 32), pl.ds(tile * LANES, LANES))
            fields = raw_fields(state, forcing, strength, ice, regimes, at)
            place(*inner, tile, PAD + top, 32, fields)
            if top == 0:
                place(*band, tile, EDGE, 32, fields)
            if top == rows - 32:
                place(*band, tiles + 1 + tile, 8, 32, fields)


def sweeps(live, coef, code_ref, rings, count, reach):
    size = 8
    lane = lane_index(size)
    first_lane = lane == 0
    last_lane = lane == LANES - 1

    def across(field, ring, top):
        parts = [row(field, tile, top) for tile in ring]
        back = [pltpu.roll(part, 1, 1) for part in parts]
        ahead = [pltpu.roll(part, LANES - 1, 1) for part in parts]
        wide = len(ring)
        return [
            jnp.where(last_lane, ahead[(i + 1) % wide], ahead[i])
            - jnp.where(first_lane, back[i - 1], back[i])
            for i in range(wide)
        ]

    def row(field, tile, top):
        return live[field, tile, pl.ds(top, size), :]

    def down(field, tile, top):
        return row(field, tile, top + 1) - row(field, tile, top - 1)

    for level in range(count):
        left = 2 * (count - level)
        for ring in rings:
            for top in reach(left - 1):
                span = pl.ds(top, size)
                for tile, du_dx, dv_dx in zip(ring, across(0, ring, top), across(1, ring, top)):
                    dv_dy = down(1, tile, top)
                    du_dy = down(0, tile, top)
                    base = coef[0, tile, span, :]
                    weak = (code_ref[tile, span, :] & (2 << level)) != 0
                    scale = base * jnp.where(weak, 0.5, 1.5)
                    half = 0.5 * (du_dx + dv_dy)
                    live[2, tile, span, :] = 0.5 * row(2, tile, top) + (scale * (du_dx + half) - base)
                    live[3, tile, span, :] = 0.5 * row(3, tile, top) + (scale * (dv_dy + half) - base)
                    live[4, tile, span, :] = 0.5 * (row(4, tile, top) + scale * (du_dy + dv_dx))
        for ring in rings:
            for top in reach(left - 2):
                span = pl.ds(top, size)
                for tile, da_dx, dt_dx in zip(ring, across(2, ring, top), across(4, ring, top)):
                    u, v = (row(0, tile, top), row(1, tile, top))
                    damp = coef[1, tile, span, :]
                    pull_x = 0.125 * (da_dx + down(4, tile, top))
                    pull_y = 0.125 * (down(3, tile, top) + dt_dx)
                    live[0, tile, span, :] = damp * (u + SPIN * v + pull_x) + coef[2, tile, span, :]
                    live[1, tile, span, :] = damp * (v - SPIN * u + pull_y) + coef[3, tile, span, :]


def rim_readers(depth, lats):
    lat, lon = both_axes()
    lat_even = lax.rem(lat, 2) == 0
    lon_even = lax.rem(lon, 2) == 0
    south = jnp.where(lat == lats - 1, 0.0, 1.0)
    north = jnp.where(lat == 0, 0.0, 1.0)

    def rim(a, b):
        return unslotted(jnp.where(lon_even, b, a), jnp.where(lon_even, a, b), depth)

    def from_north(a, b):
        return north * jnp.where(lat_even, b, a)

    def from_south(a, b):
        return south * jnp.where(lat_even, a, b)

    return rim, from_north, from_south


def block_for(route, band, target):
    return sum(jnp.where(route[band, j] == target, j, 0) for j in range(route.shape[1]))


def inner_half(block, blocks):
    return pl.multiple_of(jnp.where(block == blocks - 1, 0, HALF), HALF)


def outer_half(block, blocks):
    return pl.multiple_of(jnp.where(block == blocks - 1, HALF, 0), HALF)


def finals(live, tile, span):
    u, v, a, b, t = (live[field, tile, span, :] for field in range(5))
    return (u, v, 0.5 * (a + b), 0.5 * (a - b), 0.5 * t)


def emit(live, target, start, columns):
    span = pl.ds(pl.multiple_of(PAD + start, 8), target.shape[1])
    for tile in range(columns // LANES):
        for field, value in enumerate(finals(live, tile, span)):
            target[field, :, pl.ds(tile * LANES, LANES)] = value


def inner_kernel(count, *refs):
    inner = refs[3:]
    _, tiles, high, _ = inner[0].shape
    rows = high - 2 * PAD

    def reach(cells):
        return range(PAD + (HALF - cells) // 8 * 8, PAD + rows - HALF + cells, 8)

    sweeps(*inner, [range(tiles)], count, reach)


def sides_kernel(depth, count, blocks, table, lon_a, lon_b, *refs):
    raw, refs = refs[:5], refs[9:]
    live, band, outgoing, side = refs[0], refs[1:4], refs[4:-3], refs[-3:]
    rows, columns = raw[2].shape
    tiles = columns // LANES
    rim, _, _ = rim_readers(depth, blocks)
    own, middle = (2 * depth, LANES // 2)

    def joined(first, last, halo):
        lane = lane_index(first.shape[0])
        east = jnp.where(lane < middle, roll_to(last, middle), roll_to(halo, middle))
        east = jnp.where((lane >= middle - own) & (lane < middle + depth), east, 0.0)
        return jnp.where(lane < own, first, jnp.where(lane >= LANES - depth, halo, east))

    for field in range(5):
        for top in (0, PAD + rows):
            side[0][field, 0, pl.ds(top, PAD), :] = jnp.zeros((PAD, LANES), jnp.float32)
    for top in range(0, rows, 32):
        span = pl.ds(top, 32)
        halo = rim(lon_a[span, :], lon_b[span, :])
        first = raw_fields(*raw, (span, pl.ds(0, LANES)))
        last = raw_fields(*raw, (span, pl.ds(columns - LANES, LANES)))
        place(*side, 0, PAD + top, 32, [joined(*x) for x in zip(first, last, halo)])
        if top == 0:
            place(*band, tiles, EDGE, 32, halo)
        if top == rows - 32:
            place(*band, 2 * tiles + 1, 8, 32, halo)

    def reach(cells):
        return range(PAD + (HALF - cells) // 8 * 8, PAD + rows - HALF + cells, 8)

    sweeps(*side, [[0]], count, reach)
    lane = lane_index(16)
    for top in range(HALF, rows - HALF, 16):
        span = pl.ds(PAD + top, 16)
        for field in range(5):
            value = side[0][field, 0, span, :]
            for tile, fixed, inside in (
                (0, value, lane < depth),
                (tiles - 1, roll_to(value, middle), lane >= LANES - depth),
            ):
                live[field, tile, span, :] = jnp.where(inside, fixed, live[field, tile, span, :])
    for hop, target in enumerate(outgoing, 2):
        block = table[0, hop]
        emit(live, target, block * (rows // blocks) + inner_half(block, blocks), columns)


def outer_kernel(depth, count, blocks, table, lat_a, lat_b, *refs):
    refs = refs[4:]
    live, band, outgoing = refs[0], refs[1:4], refs[4:]
    rows, columns = (live.shape[2] - 2 * PAD, lat_a.shape[1])
    tiles = columns // LANES
    tall = rows // blocks
    rim, from_north, from_south = rim_readers(depth, blocks)
    spans = [pl.ds(depth * f, depth) for f in range(FIELDS + 1)]
    for ring, top, chosen in ((0, EDGE - depth, from_north), (tiles + 1, 40, from_south)):
        for tile in range(tiles):
            here = pl.ds(tile * LANES, LANES)
            place(*band, ring + tile, top, depth, [chosen(lat_a[s, here], lat_b[s, here]) for s in spans[:-1]])
        pair = [chosen(lat_a[spans[-1], pl.ds(c, LANES)], lat_b[spans[-1], pl.ds(c, LANES)]) for c in (0, LANES)]
        place(*band, ring + tiles, top, depth, rim(*pair))

    def reach(cells):
        return range((EDGE - cells) // 8 * 8, EDGE + HALF + cells, 8)

    sweeps(*band, [range(tiles + 1), range(tiles + 1, 2 * tiles + 2)], count, reach)
    for ring, top in ((0, 0), (tiles + 1, rows - HALF)):
        for tile in range(tiles):
            for field in range(5):
                live[field, tile, pl.ds(PAD + top, HALF), :] = band[0][field, ring + tile, pl.ds(EDGE, HALF), :]
    for hop, target in enumerate(outgoing[:-2], 2):
        block = table[0, hop]
        emit(live, target, block * tall + outer_half(block, blocks), columns)
    for half, target in enumerate(outgoing[-2:]):
        emit(live, target, table[0, 1] * tall + half * HALF, columns)


def collect_kernel(blocks, table, forcing, ice, live, *refs):
    early, (flux, out, own, sem) = refs[: blocks - 2], refs[blocks - 2 :]
    rows, columns = ice.shape
    lat = lax.axis_index("lat")
    copies = []
    for hop, part in enumerate(early, 2):
        start = inner_half(table[1, hop], blocks)
        copies.append(pltpu.make_async_copy(part, out.at[lat ^ hop, :, pl.ds(start, HALF), :], sem.at[hop]))
        copies[-1].start()
    emit(live, own, table[0, 0] * (rows // blocks), columns)
    copies.append(pltpu.make_async_copy(own, out.at[lat], sem.at[0]))
    copies[-1].start()
    for tile in range(columns // LANES):
        for top in range(0, rows, 32):
            at = (pl.ds(top, 32), pl.ds(tile * LANES, LANES))
            span = pl.ds(PAD + top, 32)
            icy = DRAG * ice[at].astype(jnp.float32)
            flux[(0, *at)] = icy * (live[0, tile, span, :] - forcing[(2, *at)])
            flux[(1, *at)] = icy * (live[1, tile, span, :] - forcing[(3, *at)])
    for copy in copies:
        copy.wait()


def gather_kernel(blocks, table, *refs):
    late, (_, out, sem) = refs[:blocks], refs[blocks:]
    lat = lax.axis_index("lat")
    copies = []
    for index, part in enumerate(late):
        hop = index + 2 if index < blocks - 2 else 1
        start = outer_half(table[1, hop], blocks) if hop > 1 else (index - blocks + 2) * HALF
        copies.append(pltpu.make_async_copy(part, out.at[lat ^ hop, :, pl.ds(start, HALF), :], sem.at[index]))
        copies[-1].start()
    for copy in copies:
        copy.wait()


def spec(space=VMEM):
    return pl.BlockSpec(memory_space=space)


def params():
    return pltpu.CompilerParams(vmem_limit_bytes=16 << 20)


def cost(flops, data):
    return pl.CostEstimate(flops=flops, bytes_accessed=data, transcendentals=0)


def lon_swaps(a, b, lons):
    near = [(i, i ^ 1) for i in range(lons)]
    far = [(i, (i + 1 if i % 2 else i - 1) % lons) for i in range(lons)]
    return lax.ppermute(a, "lon", near), lax.ppermute(b, "lon", far)


def lat_swaps(a, b, lats, lons):
    near = [(i, i ^ 1) for i in range(lats)]
    far = []
    for i in range(lats):
        for j in range(lons):
            if i in (0, lats - 1):
                far.append((i * lons + j, i * lons + (j ^ 1)))
            else:
                far.append((i * lons + j, (i + 1 if i % 2 else i - 1) * lons + j))
    return lax.ppermute(a, "lat", near), lax.ppermute(b, ("lat", "lon"), far)


def per_device(ice_state, ocean_forcing, ice_strength, ice_mask, yield_mask, ice_route):
    f32 = jnp.float32
    count = yield_mask.shape[0]
    depth = 2 * count
    rows, columns = ice_strength.shape
    lats, lons = (lax.axis_size("lat"), lax.axis_size("lon"))
    tall = rows // lats
    inputs = (ice_route, ice_state, ocean_forcing, ice_strength, ice_mask, yield_mask)
    shape = jax.ShapeDtypeStruct
    lon_rim = shape((rows, LANES), f32)
    lat_rim = shape((depth * (FIELDS + 1), columns), f32)
    tiles = columns // LANES + 1

    def fields(tiles, rows):
        return [
            shape((5, tiles, rows, LANES), f32),
            shape((4, tiles, rows, LANES), f32),
            shape((tiles, rows, LANES), jnp.int32),
        ]

    inner, band = (fields(tiles - 1, rows + 2 * PAD), fields(2 * tiles, BAND))
    side = [VMEM(x.shape, x.dtype) for x in fields(1, rows + 2 * PAD)]
    whole, half = (shape((5, tall, columns), f32), shape((5, HALF, columns), f32))
    lon_a, lon_b, lat_a, lat_b, route, *raw = pl.pallas_call(
        functools.partial(pack_kernel, depth),
        out_shape=[lon_rim] * 2 + [lat_rim] * 2 + [shape(x.shape, x.dtype) for x in inputs],
        in_specs=[spec(HBM)] * 6,
        out_specs=[spec()] * 10,
        scratch_shapes=[pltpu.SemaphoreType.DMA((6,))],
        compiler_params=params(),
        name="pack",
    )(*[pltpu.with_memory_space_constraint(x, HBM) for x in inputs])
    lon_a, lon_b = lon_swaps(lon_a, lon_b, lons)
    prepared = pl.pallas_call(
        prepare_kernel,
        out_shape=inner + band + [shape((8, LANES), jnp.int32)],
        in_specs=[spec()] * 6,
        out_specs=[spec()] * 7,
        compiler_params=params(),
        cost_estimate=cost(40 * rows * columns, 100 * rows * columns),
        name="prepare",
    )(route, *raw)
    table = prepared[6]
    live, _, _ = pl.pallas_call(
        functools.partial(inner_kernel, count),
        out_shape=inner,
        in_specs=[spec()] * 3,
        out_specs=[spec()] * 3,
        input_output_aliases={i: i for i in range(3)},
        compiler_params=params(),
        name="inner",
    )(*prepared[:3])
    lat_a, lat_b = pl.pallas_call(
        functools.partial(corner_kernel, depth),
        out_shape=[lat_rim] * 2,
        in_specs=[spec()] * 4 + [spec(pl.ANY)],
        out_specs=[spec()] * 2,
        input_output_aliases={2: 0, 3: 1},
        compiler_params=params(),
        name="corner",
    )(lon_a, lon_b, lat_a, lat_b, live)
    lat_a, lat_b = lat_swaps(lat_a, lat_b, lats, lons)

    def send(part, hop):
        return lax.ppermute(part, "lat", [(i, i ^ hop) for i in range(lats)])

    live, *rest = pl.pallas_call(
        functools.partial(sides_kernel, depth, count, lats),
        out_shape=inner[:1] + band + [half] * (lats - 2),
        in_specs=[spec()] * 12,
        out_specs=[spec()] * (2 + lats),
        scratch_shapes=side,
        input_output_aliases={8 + i: i for i in range(4)},
        compiler_params=params(),
        name="sides",
    )(table, lon_a, lon_b, *raw, live, *prepared[3:6])
    edges, early = (rest[:3], rest[3:])
    for hop in range(lats - 1, 1, -1):
        early[hop - 2] = send(early[hop - 2], hop)
    live, _, _, _, *late = pl.pallas_call(
        functools.partial(outer_kernel, depth, count, lats),
        out_shape=inner[:1] + band + [half] * lats,
        in_specs=[spec()] * 7,
        out_specs=[spec()] * (4 + lats),
        input_output_aliases={3 + i: i for i in range(4)},
        compiler_params=params(),
        name="outer",
    )(table, lat_a, lat_b, live, *edges)
    hops = [*range(2, lats), 1, 1]
    for index in (*range(lats - 3, -1, -1), lats - 2, lats - 1):
        late[index] = send(late[index], hops[index])
    result = shape((lats, *whole.shape), f32)
    flux, blocks = pl.pallas_call(
        functools.partial(collect_kernel, lats),
        out_shape=[shape((2, rows, columns), f32), result],
        in_specs=[spec()] * (2 + lats),
        out_specs=[spec(), spec(HBM)],
        scratch_shapes=[VMEM(whole.shape, f32), pltpu.SemaphoreType.DMA((lats,))],
        compiler_params=params(),
        name="collect",
    )(table, raw[1], raw[3], live, *early)
    blocks = pl.pallas_call(
        functools.partial(gather_kernel, lats),
        out_shape=result,
        in_specs=[spec()] * (1 + lats) + [spec(HBM)],
        out_specs=spec(HBM),
        scratch_shapes=[pltpu.SemaphoreType.DMA((lats,))],
        input_output_aliases={1 + lats: 0},
        compiler_params=params(),
        name="gather",
    )(table, *late, blocks)
    return flux, blocks


def solution(mesh):
    return jax.shard_map(
        per_device,
        mesh=mesh,
        in_specs=(
            P(None, "lat", "lon"),
            P(None, "lat", "lon"),
            P("lat", "lon"),
            P("lat", "lon"),
            P(None, "lat", "lon"),
            P(),
        ),
        out_specs=(P(None, "lat", "lon"), P("lat", None, None, "lon")),
        check_vma=False,
    )
```

```python
import functools
import jax
import jax.numpy as jnp
from jax import lax
from jax.experimental import pallas as pl
from jax.experimental.pallas import tpu as pltpu
from jax.sharding import PartitionSpec as P

DRAG = 0.5
SPIN = 0.15
DAMP = 0.8
LANES = 128
PAD = 8
BAND = 64
EDGE = 24
HALF = 16
FIELDS = 9
VMEM = pltpu.VMEM
HBM = pltpu.HBM


def lane_index(rows):
    return lax.broadcasted_iota(jnp.int32, (rows, LANES), 1)


def raw_fields(state, forcing, strength, ice, regimes, at):
    count = regimes.shape[0]
    s_one, s_two = (state[(2, *at)], state[(3, *at)])
    code = ice[at]
    for level in range(count):
        code = code + regimes[(level, *at)] * (2 << level)
    return [
        state[(0, *at)],
        state[(1, *at)],
        s_one + s_two,
        s_one - s_two,
        2.0 * state[(4, *at)],
        forcing[(0, *at)] + DRAG * forcing[(2, *at)],
        forcing[(1, *at)] + DRAG * forcing[(3, *at)],
        strength[at],
        code.astype(jnp.float32),
    ]


def both_axes():
    return (lax.axis_index("lat"), lax.axis_index("lon"))


def roll_to(value, shift):
    return value if shift % LANES == 0 else pltpu.roll(value, shift % LANES, 1)


def slotted(values, depth, start):
    lane = lane_index(values[0].shape[0])
    packed = roll_to(values[0], -start)
    for field in range(1, FIELDS):
        packed = jnp.where(lane >= depth * field, roll_to(values[field], depth * field - start), packed)
    return packed


def unslotted(west, east, depth):
    lane = lane_index(west.shape[0])
    fields = []
    for field in range(FIELDS):
        right = roll_to(east, -depth * field)
        left = roll_to(west, -depth * (field + 1))
        fields.append(jnp.where(lane < depth, right, jnp.where(lane >= LANES - depth, left, 0.0)))
    return fields


def pack_kernel(depth, *refs):
    sources, (lon_a, lon_b, lat_a, lat_b), held, sem = refs[:6], refs[6:10], refs[10:16], refs[16]
    rows, columns = held[3].shape
    waves = 2
    step = rows // waves
    copies = []
    for wave in range(waves):
        for source, target in zip(sources[1:], held[1:]):
            at = (slice(None),) * (len(source.shape) - 2) + (pl.ds(wave * step, step), slice(None))
            copies.append((wave, pltpu.make_async_copy(source.at[at], target.at[at], sem.at[wave])))
    copies.append((waves - 1, pltpu.make_async_copy(sources[0], held[0], sem.at[waves])))
    for _, copy in copies:
        copy.start()
    raw = held[1:]
    lat, lon = both_axes()
    lat_even = lax.rem(lat, 2) == 0
    lon_even = lax.rem(lon, 2) == 0
    for wave in range(waves):
        for index, copy in copies:
            if index == wave:
                copy.wait()
        for top in range(wave * step, (wave + 1) * step, 32):
            span = pl.ds(top, 32)
            first = slotted(raw_fields(*raw, (span, pl.ds(0, LANES))), depth, 0)
            last = slotted(raw_fields(*raw, (span, pl.ds(columns - LANES, LANES))), depth, LANES - depth)
            lon_a[span, :] = jnp.where(lon_even, last, first)
            lon_b[span, :] = jnp.where(lon_even, first, last)
    for column in range(0, columns, LANES):
        here = pl.ds(column, LANES)
        first = raw_fields(*raw, (pl.ds(0, 16), here))
        last = raw_fields(*raw, (pl.ds(rows - 16, 16), here))
        for field in range(FIELDS):
            span = pl.ds(depth * field, depth)
            one, two = (first[field][:depth], last[field][16 - depth :])
            lat_a[span, here] = jnp.where(lat_even, two, one)
            lat_b[span, here] = jnp.where(lat_even, one, two)


def corner_kernel(depth, lon_a, lon_b, lat_a, lat_b, after, out_a, out_b):
    rows = lon_a.shape[0]
    lat_even = lax.rem(lax.axis_index("lat"), 2) == 0
    span = pl.ds(depth * FIELDS, depth)
    for source, column in ((lon_a, 0), (lon_b, LANES)):
        first = source[pl.ds(0, 16), :][:depth]
        last = source[pl.ds(rows - 16, 16), :][16 - depth :]
        out_a[span, pl.ds(column, LANES)] = jnp.where(lat_even, last, first)
        out_b[span, pl.ds(column, LANES)] = jnp.where(lat_even, first, last)


def evolved(fields):
    u, v, a, b, t, fx, fy, strong, code = fields
    code = code.astype(jnp.int32)
    icy = (code & 1).astype(jnp.float32)
    kept = [u, v, icy * a, icy * b, icy * t]
    scales = [0.25 * icy * strong, DAMP * icy, (0.5 * DAMP) * icy * fx, (0.5 * DAMP) * icy * fy]
    return kept, scales, code


def place(live, coef, code_ref, tile, top, size, fields):
    span = pl.ds(top, size)
    kept, scales, code = evolved(fields)
    for field, value in enumerate(kept):
        live[field, tile, span, :] = value
    for field, value in enumerate(scales):
        coef[field, tile, span, :] = value
    code_ref[tile, span, :] = code


def prepare_kernel(depth, route, state, forcing, strength, ice, regimes, *refs):
    inner, band, table, side = refs[:3], refs[3:6], refs[6], refs[7:]
    lat = lax.axis_index("lat")
    line, lane = (lax.broadcasted_iota(jnp.int32, table.shape, axis) for axis in range(2))
    found = jnp.zeros(table.shape, jnp.int32)
    for hop in range(route.shape[0]):
        other = lat ^ hop
        for index, block in enumerate((block_for(route, lat, other), block_for(route, other, lat))):
            found = jnp.where((line == index) & (lane == hop), block, found)
    table[...] = found
    rows, columns = strength.shape
    tiles = columns // LANES

    def clear(refs, tile, top, size):
        span = pl.ds(top, size)
        zero = jnp.zeros((size, LANES), jnp.float32)
        for ref in refs[:2]:
            for field in range(ref.shape[0]):
                ref[field, tile, span, :] = zero
        refs[2][tile, span, :] = zero.astype(jnp.int32)

    for tile in range(tiles):
        clear(inner, tile, 0, PAD)
        clear(inner, tile, PAD + rows, PAD)
    for tile in range(tiles + 1):
        clear(band, tile, 0, EDGE)
        clear(band, tile, EDGE + 32, BAND - EDGE - 32)
        clear(band, tiles + 1 + tile, 0, 8)
        clear(band, tiles + 1 + tile, 40, BAND - 40)
    for field in range(5):
        for top in (0, PAD + rows):
            side[0][field, 0, pl.ds(top, PAD), :] = jnp.zeros((PAD, LANES), jnp.float32)
    lane = lane_index(32)
    own, middle = (2 * depth, LANES // 2)
    east = (lane >= middle - own) & (lane < middle)
    for top in range(0, rows, 32):
        ends = []
        for tile in range(tiles):
            at = (pl.ds(top, 32), pl.ds(tile * LANES, LANES))
            fields = raw_fields(state, forcing, strength, ice, regimes, at)
            place(*inner, tile, PAD + top, 32, fields)
            if top == 0:
                place(*band, tile, EDGE, 32, fields)
            if top == rows - 32:
                place(*band, tiles + 1 + tile, 8, 32, fields)
            if tile in (0, tiles - 1):
                ends.append(fields)
        both = zip(ends[0], ends[-1])
        joined = [jnp.where(lane < own, x, jnp.where(east, roll_to(y, middle), 0.0)) for x, y in both]
        place(*side, 0, PAD + top, 32, joined)


def sweeps(live, coef, code_ref, rings, count, reach):
    size = 8
    lane = lane_index(size)
    first_lane = lane == 0
    last_lane = lane == LANES - 1

    def across(field, ring, top):
        parts = [row(field, tile, top) for tile in ring]
        back = [pltpu.roll(part, 1, 1) for part in parts]
        ahead = [pltpu.roll(part, LANES - 1, 1) for part in parts]
        wide = len(ring)
        return [
            jnp.where(last_lane, ahead[(i + 1) % wide], ahead[i])
            - jnp.where(first_lane, back[i - 1], back[i])
            for i in range(wide)
        ]

    def row(field, tile, top):
        return live[field, tile, pl.ds(top, size), :]

    def down(field, tile, top):
        return row(field, tile, top + 1) - row(field, tile, top - 1)

    for level in range(count):
        left = 2 * (count - level)
        for ring in rings:
            for top in reach(left - 1):
                span = pl.ds(top, size)
                for tile, du_dx, dv_dx in zip(ring, across(0, ring, top), across(1, ring, top)):
                    dv_dy = down(1, tile, top)
                    du_dy = down(0, tile, top)
                    base = coef[0, tile, span, :]
                    weak = (code_ref[tile, span, :] & (2 << level)) != 0
                    scale = base * jnp.where(weak, 0.5, 1.5)
                    half = 0.5 * (du_dx + dv_dy)
                    live[2, tile, span, :] = 0.5 * row(2, tile, top) + (scale * (du_dx + half) - base)
                    live[3, tile, span, :] = 0.5 * row(3, tile, top) + (scale * (dv_dy + half) - base)
                    live[4, tile, span, :] = 0.5 * (row(4, tile, top) + scale * (du_dy + dv_dx))
        for ring in rings:
            for top in reach(left - 2):
                span = pl.ds(top, size)
                for tile, da_dx, dt_dx in zip(ring, across(2, ring, top), across(4, ring, top)):
                    u, v = (row(0, tile, top), row(1, tile, top))
                    damp = coef[1, tile, span, :]
                    pull_x = 0.125 * (da_dx + down(4, tile, top))
                    pull_y = 0.125 * (down(3, tile, top) + dt_dx)
                    live[0, tile, span, :] = damp * (u + SPIN * v + pull_x) + coef[2, tile, span, :]
                    live[1, tile, span, :] = damp * (v - SPIN * u + pull_y) + coef[3, tile, span, :]


def rim_readers(depth, lats):
    lat, lon = both_axes()
    lat_even = lax.rem(lat, 2) == 0
    lon_even = lax.rem(lon, 2) == 0
    south = jnp.where(lat == lats - 1, 0.0, 1.0)
    north = jnp.where(lat == 0, 0.0, 1.0)

    def rim(a, b):
        return unslotted(jnp.where(lon_even, b, a), jnp.where(lon_even, a, b), depth)

    def from_north(a, b):
        return north * jnp.where(lat_even, b, a)

    def from_south(a, b):
        return south * jnp.where(lat_even, a, b)

    return rim, from_north, from_south


def block_for(route, band, target):
    return sum(jnp.where(route[band, j] == target, j, 0) for j in range(route.shape[1]))


def soon(blocks):
    return [*range(blocks - 1, 0, -1)]


def later(blocks):
    return [(hop, None) for hop in range(1, blocks)]


def inner_half(block, blocks):
    return pl.multiple_of(jnp.where(block == blocks - 1, 0, HALF), HALF)


def outer_half(block, blocks):
    return pl.multiple_of(jnp.where(block == blocks - 1, HALF, 0), HALF)


def finals(live, tile, span):
    u, v, a, b, t = (live[field, tile, span, :] for field in range(5))
    return (u, v, 0.5 * (a + b), 0.5 * (a - b), 0.5 * t)


def emit(live, target, start, columns):
    span = pl.ds(pl.multiple_of(PAD + start, 8), target.shape[1])
    for tile in range(columns // LANES):
        for field, value in enumerate(finals(live, tile, span)):
            target[field, :, pl.ds(tile * LANES, LANES)] = value


def inner_kernel(count, *refs):
    inner = refs[3:]
    _, tiles, high, _ = inner[0].shape
    rows = high - 2 * PAD

    def reach(cells):
        return range(PAD + (HALF - cells) // 8 * 8, PAD + rows - HALF + cells, 8)

    sweeps(*inner, [range(tiles)], count, reach)


def sides_kernel(depth, count, blocks, table, lon_a, lon_b, *refs):
    refs = refs[7:]
    live, band, side, outgoing = refs[0], refs[1:4], refs[4:7], refs[7:]
    rows = lon_a.shape[0]
    tiles = live.shape[1]
    columns = tiles * LANES
    rim, _, _ = rim_readers(depth, blocks)
    middle = LANES // 2
    lane = lane_index(32)
    west = lane >= LANES - depth
    east = (lane >= middle) & (lane < middle + depth)
    for top in range(0, rows, 32):
        span = pl.ds(top, 32)
        halo = rim(lon_a[span, :], lon_b[span, :])
        if top == 0:
            place(*band, tiles, EDGE, 32, halo)
        if top == rows - 32:
            place(*band, 2 * tiles + 1, 8, 32, halo)
        span = pl.ds(PAD + top, 32)
        kept, scales, code = evolved(halo)
        for ref, values in ((side[0], kept), (side[1], scales)):
            for field, value in enumerate(values):
                value = jnp.where(west, value, roll_to(value, middle))
                ref[field, 0, span, :] = jnp.where(west | east, value, ref[field, 0, span, :])
        code = jnp.where(west, code, roll_to(code, middle))
        side[2][0, span, :] = jnp.where(west | east, code, side[2][0, span, :])

    def reach(cells):
        return range(PAD + (HALF - cells) // 8 * 8, PAD + rows - HALF + cells, 8)

    sweeps(*side, [[0]], count, reach)
    lane = lane_index(16)
    for top in range(HALF, rows - HALF, 16):
        span = pl.ds(PAD + top, 16)
        for field in range(5):
            value = side[0][field, 0, span, :]
            for tile, fixed, inside in (
                (0, value, lane < depth),
                (tiles - 1, roll_to(value, middle), lane >= LANES - depth),
            ):
                live[field, tile, span, :] = jnp.where(inside, fixed, live[field, tile, span, :])
    for hop, target in zip(soon(blocks), outgoing):
        block = table[0, hop]
        emit(live, target, block * (rows // blocks) + inner_half(block, blocks), columns)


def outer_kernel(depth, count, blocks, table, lat_b, lat_a, *refs):
    refs = refs[4:]
    live, band, outgoing = refs[0], refs[1:4], refs[4:]
    rows, columns = (live.shape[2] - 2 * PAD, lat_a.shape[1])
    tiles = columns // LANES
    tall = rows // blocks
    rim, from_north, from_south = rim_readers(depth, blocks)
    spans = [pl.ds(depth * f, depth) for f in range(FIELDS + 1)]
    for ring, top, chosen in ((0, EDGE - depth, from_north), (tiles + 1, 40, from_south)):
        for tile in range(tiles):
            here = pl.ds(tile * LANES, LANES)
            place(*band, ring + tile, top, depth, [chosen(lat_a[s, here], lat_b[s, here]) for s in spans[:-1]])
        pair = [chosen(lat_a[spans[-1], pl.ds(c, LANES)], lat_b[spans[-1], pl.ds(c, LANES)]) for c in (0, LANES)]
        place(*band, ring + tiles, top, depth, rim(*pair))

    def reach(cells):
        return range((EDGE - cells) // 8 * 8, EDGE + HALF + cells, 8)

    sweeps(*band, [range(tiles + 1), range(tiles + 1, 2 * tiles + 2)], count, reach)
    for ring, top in ((0, 0), (tiles + 1, rows - HALF)):
        for tile in range(tiles):
            for field in range(5):
                live[field, tile, pl.ds(PAD + top, HALF), :] = band[0][field, ring + tile, pl.ds(EDGE, HALF), :]
    for (hop, half), target in zip(later(blocks), outgoing):
        block = table[0, hop]
        start = outer_half(block, blocks) if half is None else half * HALF
        emit(live, target, block * tall + start, columns)


def collect_kernel(blocks, table, forcing, ice, live, *refs):
    early, (flux, out, own, sem) = refs[:-4], refs[-4:]
    rows, columns = ice.shape
    lat = lax.axis_index("lat")
    copies = []
    for hop, part in zip(soon(blocks), early):
        start = inner_half(table[1, hop], blocks)
        copies.append(pltpu.make_async_copy(part, out.at[lat ^ hop, :, pl.ds(start, HALF), :], sem.at[hop]))
        copies[-1].start()
    emit(live, own, table[0, 0] * (rows // blocks), columns)
    copies.append(pltpu.make_async_copy(own, out.at[lat], sem.at[0]))
    copies[-1].start()
    for tile in range(columns // LANES):
        for top in range(0, rows, 32):
            at = (pl.ds(top, 32), pl.ds(tile * LANES, LANES))
            span = pl.ds(PAD + top, 32)
            icy = DRAG * ice[at].astype(jnp.float32)
            flux[(0, *at)] = icy * (live[0, tile, span, :] - forcing[(2, *at)])
            flux[(1, *at)] = icy * (live[1, tile, span, :] - forcing[(3, *at)])
    for copy in copies:
        copy.wait()


def gather_kernel(blocks, table, *refs):
    late, (_, out, sem) = refs[:-3], refs[-3:]
    lat = lax.axis_index("lat")
    copies = []
    for index, ((hop, half), part) in enumerate(zip(later(blocks), late)):
        start = outer_half(table[1, hop], blocks) if half is None else half * HALF
        copies.append(pltpu.make_async_copy(part, out.at[lat ^ hop, :, pl.ds(start, HALF), :], sem.at[index]))
        copies[-1].start()
    for copy in copies:
        copy.wait()


def spec(space=VMEM):
    return pl.BlockSpec(memory_space=space)


def params():
    return pltpu.CompilerParams(vmem_limit_bytes=16 << 20)


def cost(flops, data):
    return pl.CostEstimate(flops=flops, bytes_accessed=data, transcendentals=0)


def lon_swaps(a, b, lons):
    near = [(i, i ^ 1) for i in range(lons)]
    far = [(i, (i + 1 if i % 2 else i - 1) % lons) for i in range(lons)]
    return lax.ppermute(a, "lon", near), lax.ppermute(b, "lon", far)


def lat_swaps(a, b, lats, lons):
    near = [(i, i ^ 1) for i in range(lats)]
    far = []
    for i in range(lats):
        for j in range(lons):
            if i in (0, lats - 1):
                far.append((i * lons + j, i * lons + (j ^ 1)))
            else:
                far.append((i * lons + j, (i + 1 if i % 2 else i - 1) * lons + j))
    return lax.ppermute(a, "lat", near), lax.ppermute(b, ("lat", "lon"), far)


def per_device(ice_state, ocean_forcing, ice_strength, ice_mask, yield_mask, ice_route):
    f32 = jnp.float32
    count = yield_mask.shape[0]
    depth = 2 * count
    rows, columns = ice_strength.shape
    lats, lons = (lax.axis_size("lat"), lax.axis_size("lon"))
    tall = rows // lats
    inputs = (ice_route, ice_state, ocean_forcing, ice_strength, ice_mask, yield_mask)
    shape = jax.ShapeDtypeStruct
    lon_rim = shape((rows, LANES), f32)
    lat_rim = shape((depth * (FIELDS + 1), columns), f32)
    tiles = columns // LANES + 1

    def fields(tiles, rows):
        return [
            shape((5, tiles, rows, LANES), f32),
            shape((4, tiles, rows, LANES), f32),
            shape((tiles, rows, LANES), jnp.int32),
        ]

    inner, band = (fields(tiles - 1, rows + 2 * PAD), fields(2 * tiles, BAND))
    side = fields(1, rows + 2 * PAD)
    whole, half = (shape((5, tall, columns), f32), shape((5, HALF, columns), f32))
    lon_a, lon_b, lat_a, lat_b, route, *raw = pl.pallas_call(
        functools.partial(pack_kernel, depth),
        out_shape=[lon_rim] * 2 + [lat_rim] * 2 + [shape(x.shape, x.dtype) for x in inputs],
        in_specs=[spec(HBM)] * 6,
        out_specs=[spec()] * 10,
        scratch_shapes=[pltpu.SemaphoreType.DMA((3,))],
        compiler_params=params(),
        name="pack",
    )(*[pltpu.with_memory_space_constraint(x, HBM) for x in inputs])
    lon_a, lon_b = lon_swaps(lon_a, lon_b, lons)
    prepared = pl.pallas_call(
        functools.partial(prepare_kernel, depth),
        out_shape=inner + band + [shape((8, LANES), jnp.int32)] + side,
        in_specs=[spec()] * 6,
        out_specs=[spec()] * 10,
        compiler_params=params(),
        cost_estimate=cost(40 * rows * columns, 100 * rows * columns),
        name="prepare",
    )(route, *raw)
    table = prepared[6]
    live, _, _ = pl.pallas_call(
        functools.partial(inner_kernel, count),
        out_shape=inner,
        in_specs=[spec()] * 3,
        out_specs=[spec()] * 3,
        input_output_aliases={i: i for i in range(3)},
        compiler_params=params(),
        name="inner",
    )(*prepared[:3])
    lat_a, lat_b = pl.pallas_call(
        functools.partial(corner_kernel, depth),
        out_shape=[lat_rim] * 2,
        in_specs=[spec()] * 4 + [spec(pl.ANY)],
        out_specs=[spec()] * 2,
        input_output_aliases={2: 0, 3: 1},
        compiler_params=params(),
        name="corner",
    )(lon_a, lon_b, lat_a, lat_b, live)
    lat_a, lat_b = lat_swaps(lat_a, lat_b, lats, lons)

    def send(part, hop):
        return lax.ppermute(part, "lat", [(i, i ^ hop) for i in range(lats)])

    live, *rest = pl.pallas_call(
        functools.partial(sides_kernel, depth, count, lats),
        out_shape=inner[:1] + band + side + [half] * len(soon(lats)),
        in_specs=[spec()] * 10,
        out_specs=[spec()] * (7 + len(soon(lats))),
        input_output_aliases={3 + i: i for i in range(7)},
        compiler_params=params(),
        name="sides",
    )(table, lon_a, lon_b, live, *prepared[3:6], *prepared[7:])
    edges, early = (rest[:3], rest[6:])
    early = [send(part, hop) for hop, part in zip(soon(lats), early)]
    live, _, _, _, *late = pl.pallas_call(
        functools.partial(outer_kernel, depth, count, lats),
        out_shape=inner[:1] + band + [half] * len(later(lats)),
        in_specs=[spec()] * 7,
        out_specs=[spec()] * (4 + len(later(lats))),
        input_output_aliases={3 + i: i for i in range(4)},
        compiler_params=params(),
        name="outer",
    )(table, lat_b, lat_a, live, *edges)
    late = [send(part, hop) for (hop, _), part in zip(later(lats), late)]
    result = shape((lats, *whole.shape), f32)
    flux, blocks = pl.pallas_call(
        functools.partial(collect_kernel, lats),
        out_shape=[shape((2, rows, columns), f32), result],
        in_specs=[spec()] * (4 + len(early)),
        out_specs=[spec(), spec(HBM)],
        scratch_shapes=[VMEM(whole.shape, f32), pltpu.SemaphoreType.DMA((lats,))],
        compiler_params=params(),
        name="collect",
    )(table, raw[1], raw[3], live, *early)
    blocks = pl.pallas_call(
        functools.partial(gather_kernel, lats),
        out_shape=result,
        in_specs=[spec()] * (1 + len(late)) + [spec(HBM)],
        out_specs=spec(HBM),
        scratch_shapes=[pltpu.SemaphoreType.DMA((len(late),))],
        input_output_aliases={1 + len(late): 0},
        compiler_params=params(),
        name="gather",
    )(table, *late, blocks)
    return flux, blocks


def solution(mesh):
    return jax.shard_map(
        per_device,
        mesh=mesh,
        in_specs=(
            P(None, "lat", "lon"),
            P(None, "lat", "lon"),
            P("lat", "lon"),
            P("lat", "lon"),
            P(None, "lat", "lon"),
            P(),
        ),
        out_specs=(P(None, "lat", "lon"), P("lat", None, None, "lon")),
        check_vma=False,
    )
```

```python
import functools
import jax
import jax.numpy as jnp
from jax import lax
from jax.experimental import pallas as pl
from jax.experimental.pallas import tpu as pltpu
from jax.sharding import PartitionSpec as P

DRAG = 0.5
SPIN = 0.15
DAMP = 0.8
LANES = 128
PAD = 8
BAND = 64
EDGE = 24
HALF = 16
FIELDS = 9
VMEM = pltpu.VMEM
HBM = pltpu.HBM


def lane_index(rows):
    return lax.broadcasted_iota(jnp.int32, (rows, LANES), 1)


def raw_fields(state, forcing, strength, ice, regimes, at):
    count = regimes.shape[0]
    s_one, s_two = (state[(2, *at)], state[(3, *at)])
    code = ice[at]
    for level in range(count):
        code = code + regimes[(level, *at)] * (2 << level)
    return [
        state[(0, *at)],
        state[(1, *at)],
        s_one + s_two,
        s_one - s_two,
        2.0 * state[(4, *at)],
        forcing[(0, *at)] + DRAG * forcing[(2, *at)],
        forcing[(1, *at)] + DRAG * forcing[(3, *at)],
        strength[at],
        code.astype(jnp.float32),
    ]


def both_axes():
    return (lax.axis_index("lat"), lax.axis_index("lon"))


def roll_to(value, shift):
    return value if shift % LANES == 0 else pltpu.roll(value, shift % LANES, 1)


def slotted(values, depth, start):
    lane = lane_index(values[0].shape[0])
    packed = roll_to(values[0], -start)
    for field in range(1, FIELDS):
        packed = jnp.where(lane >= depth * field, roll_to(values[field], depth * field - start), packed)
    return packed


def unslotted(west, east, depth):
    lane = lane_index(west.shape[0])
    fields = []
    for field in range(FIELDS):
        right = roll_to(east, -depth * field)
        left = roll_to(west, -depth * (field + 1))
        fields.append(jnp.where(lane < depth, right, jnp.where(lane >= LANES - depth, left, 0.0)))
    return fields


def pack_kernel(depth, *refs):
    sources, (lon_a, lon_b, lat_a, lat_b), held, sem = refs[:6], refs[6:10], refs[10:16], refs[16]
    rows, columns = held[3].shape
    waves = 2
    step = rows // waves
    copies = []
    for wave in range(waves):
        for source, target in zip(sources[1:], held[1:]):
            at = (slice(None),) * (len(source.shape) - 2) + (pl.ds(wave * step, step), slice(None))
            copies.append((wave, pltpu.make_async_copy(source.at[at], target.at[at], sem.at[wave])))
    copies.append((waves - 1, pltpu.make_async_copy(sources[0], held[0], sem.at[waves])))
    for _, copy in copies:
        copy.start()
    raw = held[1:]
    lat, lon = both_axes()
    lat_even = lax.rem(lat, 2) == 0
    lon_even = lax.rem(lon, 2) == 0
    for wave in range(waves):
        for index, copy in copies:
            if index == wave:
                copy.wait()
        for top in range(wave * step, (wave + 1) * step, 32):
            span = pl.ds(top, 32)
            first = slotted(raw_fields(*raw, (span, pl.ds(0, LANES))), depth, 0)
            last = slotted(raw_fields(*raw, (span, pl.ds(columns - LANES, LANES))), depth, LANES - depth)
            lon_a[span, :] = jnp.where(lon_even, last, first)
            lon_b[span, :] = jnp.where(lon_even, first, last)
    for column in range(0, columns, LANES):
        here = pl.ds(column, LANES)
        first = raw_fields(*raw, (pl.ds(0, 16), here))
        last = raw_fields(*raw, (pl.ds(rows - 16, 16), here))
        for field in range(FIELDS):
            span = pl.ds(depth * field, depth)
            one, two = (first[field][:depth], last[field][16 - depth :])
            lat_a[span, here] = jnp.where(lat_even, two, one)
            lat_b[span, here] = jnp.where(lat_even, one, two)


def corner_kernel(depth, lon_a, lon_b, lat_a, lat_b, after, out_a, out_b):
    rows = lon_a.shape[0]
    lat_even = lax.rem(lax.axis_index("lat"), 2) == 0
    span = pl.ds(depth * FIELDS, depth)
    for source, column in ((lon_a, 0), (lon_b, LANES)):
        first = source[pl.ds(0, 16), :][:depth]
        last = source[pl.ds(rows - 16, 16), :][16 - depth :]
        out_a[span, pl.ds(column, LANES)] = jnp.where(lat_even, last, first)
        out_b[span, pl.ds(column, LANES)] = jnp.where(lat_even, first, last)


def evolved(fields):
    u, v, a, b, t, fx, fy, strong, code = fields
    code = code.astype(jnp.int32)
    icy = (code & 1).astype(jnp.float32)
    kept = [u, v, icy * a, icy * b, icy * t]
    scales = [0.25 * icy * strong, DAMP * icy, (0.5 * DAMP) * icy * fx, (0.5 * DAMP) * icy * fy]
    return kept, scales, code


def place(live, coef, code_ref, tile, top, size, fields):
    span = pl.ds(top, size)
    kept, scales, code = evolved(fields)
    for field, value in enumerate(kept):
        live[field, tile, span, :] = value
    for field, value in enumerate(scales):
        coef[field, tile, span, :] = value
    code_ref[tile, span, :] = code


def prepare_kernel(depth, route, state, forcing, strength, ice, regimes, *refs):
    inner, band, table, side = refs[:3], refs[3:6], refs[6], refs[7:]
    lat = lax.axis_index("lat")
    line, lane = (lax.broadcasted_iota(jnp.int32, table.shape, axis) for axis in range(2))
    found = jnp.zeros(table.shape, jnp.int32)
    for hop in range(route.shape[0]):
        other = lat ^ hop
        for index, block in enumerate((block_for(route, lat, other), block_for(route, other, lat))):
            found = jnp.where((line == index) & (lane == hop), block, found)
    table[...] = found
    rows, columns = strength.shape
    tiles = columns // LANES

    def clear(refs, tile, top, size):
        span = pl.ds(top, size)
        zero = jnp.zeros((size, LANES), jnp.float32)
        for ref in refs[:2]:
            for field in range(ref.shape[0]):
                ref[field, tile, span, :] = zero
        refs[2][tile, span, :] = zero.astype(jnp.int32)

    for tile in range(tiles):
        clear(inner, tile, 0, PAD)
        clear(inner, tile, PAD + rows, PAD)
    for tile in range(tiles + 1):
        clear(band, tile, 0, EDGE)
        clear(band, tile, EDGE + 32, BAND - EDGE - 32)
        clear(band, tiles + 1 + tile, 0, 8)
        clear(band, tiles + 1 + tile, 40, BAND - 40)
    for field in range(5):
        for top in (0, PAD + rows):
            side[0][field, 0, pl.ds(top, PAD), :] = jnp.zeros((PAD, LANES), jnp.float32)
    lane = lane_index(32)
    own, middle = (2 * depth, LANES // 2)
    east = (lane >= middle - own) & (lane < middle)
    for top in range(0, rows, 32):
        ends = []
        for tile in range(tiles):
            at = (pl.ds(top, 32), pl.ds(tile * LANES, LANES))
            fields = raw_fields(state, forcing, strength, ice, regimes, at)
            place(*inner, tile, PAD + top, 32, fields)
            if top == 0:
                place(*band, tile, EDGE, 32, fields)
            if top == rows - 32:
                place(*band, tiles + 1 + tile, 8, 32, fields)
            if tile in (0, tiles - 1):
                ends.append(fields)
        both = zip(ends[0], ends[-1])
        joined = [jnp.where(lane < own, x, jnp.where(east, roll_to(y, middle), 0.0)) for x, y in both]
        place(*side, 0, PAD + top, 32, joined)


def sweeps(live, coef, code_ref, rings, count, reach):
    size = 8
    lane = lane_index(size)
    first_lane = lane == 0
    last_lane = lane == LANES - 1

    def across(field, ring, top):
        parts = [row(field, tile, top) for tile in ring]
        back = [pltpu.roll(part, 1, 1) for part in parts]
        ahead = [pltpu.roll(part, LANES - 1, 1) for part in parts]
        wide = len(ring)
        return [
            jnp.where(last_lane, ahead[(i + 1) % wide], ahead[i])
            - jnp.where(first_lane, back[i - 1], back[i])
            for i in range(wide)
        ]

    def row(field, tile, top):
        return live[field, tile, pl.ds(top, size), :]

    def down(field, tile, top):
        return row(field, tile, top + 1) - row(field, tile, top - 1)

    for level in range(count):
        left = 2 * (count - level)
        for ring in rings:
            for top in reach(left - 1):
                span = pl.ds(top, size)
                for tile, du_dx, dv_dx in zip(ring, across(0, ring, top), across(1, ring, top)):
                    dv_dy = down(1, tile, top)
                    du_dy = down(0, tile, top)
                    base = coef[0, tile, span, :]
                    weak = (code_ref[tile, span, :] & (2 << level)) != 0
                    scale = base * jnp.where(weak, 0.5, 1.5)
                    half = 0.5 * (du_dx + dv_dy)
                    live[2, tile, span, :] = 0.5 * row(2, tile, top) + (scale * (du_dx + half) - base)
                    live[3, tile, span, :] = 0.5 * row(3, tile, top) + (scale * (dv_dy + half) - base)
                    live[4, tile, span, :] = 0.5 * (row(4, tile, top) + scale * (du_dy + dv_dx))
        for ring in rings:
            for top in reach(left - 2):
                span = pl.ds(top, size)
                for tile, da_dx, dt_dx in zip(ring, across(2, ring, top), across(4, ring, top)):
                    u, v = (row(0, tile, top), row(1, tile, top))
                    damp = coef[1, tile, span, :]
                    pull_x = 0.125 * (da_dx + down(4, tile, top))
                    pull_y = 0.125 * (down(3, tile, top) + dt_dx)
                    live[0, tile, span, :] = damp * (u + SPIN * v + pull_x) + coef[2, tile, span, :]
                    live[1, tile, span, :] = damp * (v - SPIN * u + pull_y) + coef[3, tile, span, :]


def rim_readers(depth, lats):
    lat, lon = both_axes()
    lat_even = lax.rem(lat, 2) == 0
    lon_even = lax.rem(lon, 2) == 0
    south = jnp.where(lat == lats - 1, 0.0, 1.0)
    north = jnp.where(lat == 0, 0.0, 1.0)

    def rim(a, b):
        return unslotted(jnp.where(lon_even, b, a), jnp.where(lon_even, a, b), depth)

    def from_north(a, b):
        return north * jnp.where(lat_even, b, a)

    def from_south(a, b):
        return south * jnp.where(lat_even, a, b)

    return rim, from_north, from_south


def block_for(route, band, target):
    return sum(jnp.where(route[band, j] == target, j, 0) for j in range(route.shape[1]))


def soon(blocks):
    return [*range(blocks - 1, 0, -1)]


def later(blocks):
    return [2, 1, *range(3, blocks)]


def inner_half(block, blocks):
    return pl.multiple_of(jnp.where(block == blocks - 1, 0, HALF), HALF)


def outer_half(block, blocks):
    return pl.multiple_of(jnp.where(block == blocks - 1, HALF, 0), HALF)


def finals(live, tile, span):
    u, v, a, b, t = (live[field, tile, span, :] for field in range(5))
    return (u, v, 0.5 * (a + b), 0.5 * (a - b), 0.5 * t)


def emit(live, target, start, columns):
    span = pl.ds(pl.multiple_of(PAD + start, 8), target.shape[1])
    for tile in range(columns // LANES):
        for field, value in enumerate(finals(live, tile, span)):
            target[field, :, pl.ds(tile * LANES, LANES)] = value


def inner_kernel(count, *refs):
    inner = refs[3:]
    _, tiles, high, _ = inner[0].shape
    rows = high - 2 * PAD

    def reach(cells):
        return range(PAD + (HALF - cells) // 8 * 8, PAD + rows - HALF + cells, 8)

    sweeps(*inner, [range(tiles)], count, reach)


def sides_kernel(depth, count, blocks, table, lon_a, lon_b, *refs):
    refs = refs[7:]
    live, band, side, outgoing = refs[0], refs[1:4], refs[4:7], refs[7:]
    rows = lon_a.shape[0]
    tiles = live.shape[1]
    columns = tiles * LANES
    rim, _, _ = rim_readers(depth, blocks)
    middle = LANES // 2
    lane = lane_index(32)
    west = lane >= LANES - depth
    east = (lane >= middle) & (lane < middle + depth)
    for top in range(0, rows, 32):
        span = pl.ds(top, 32)
        halo = rim(lon_a[span, :], lon_b[span, :])
        if top == 0:
            place(*band, tiles, EDGE, 32, halo)
        if top == rows - 32:
            place(*band, 2 * tiles + 1, 8, 32, halo)
        span = pl.ds(PAD + top, 32)
        kept, scales, code = evolved(halo)
        for ref, values in ((side[0], kept), (side[1], scales)):
            for field, value in enumerate(values):
                value = jnp.where(west, value, roll_to(value, middle))
                ref[field, 0, span, :] = jnp.where(west | east, value, ref[field, 0, span, :])
        code = jnp.where(west, code, roll_to(code, middle))
        side[2][0, span, :] = jnp.where(west | east, code, side[2][0, span, :])

    def reach(cells):
        return range(PAD + (HALF - cells) // 8 * 8, PAD + rows - HALF + cells, 8)

    sweeps(*side, [[0]], count, reach)
    lane = lane_index(16)
    for top in range(HALF, rows - HALF, 16):
        span = pl.ds(PAD + top, 16)
        for field in range(5):
            value = side[0][field, 0, span, :]
            for tile, fixed, inside in (
                (0, value, lane < depth),
                (tiles - 1, roll_to(value, middle), lane >= LANES - depth),
            ):
                live[field, tile, span, :] = jnp.where(inside, fixed, live[field, tile, span, :])
    for hop, target in zip(soon(blocks), outgoing):
        block = table[0, hop]
        emit(live, target, block * (rows // blocks) + inner_half(block, blocks), columns)


def outer_kernel(depth, count, blocks, table, lat_b, lat_a, *refs):
    refs = refs[4:]
    live, band, outgoing = refs[0], refs[1:4], refs[4:]
    rows, columns = (live.shape[2] - 2 * PAD, lat_a.shape[1])
    tiles = columns // LANES
    tall = rows // blocks
    rim, from_north, from_south = rim_readers(depth, blocks)
    spans = [pl.ds(depth * f, depth) for f in range(FIELDS + 1)]
    for ring, top, chosen in ((0, EDGE - depth, from_north), (tiles + 1, 40, from_south)):
        for tile in range(tiles):
            here = pl.ds(tile * LANES, LANES)
            place(*band, ring + tile, top, depth, [chosen(lat_a[s, here], lat_b[s, here]) for s in spans[:-1]])
        pair = [chosen(lat_a[spans[-1], pl.ds(c, LANES)], lat_b[spans[-1], pl.ds(c, LANES)]) for c in (0, LANES)]
        place(*band, ring + tiles, top, depth, rim(*pair))

    def reach(cells):
        return range((EDGE - cells) // 8 * 8, EDGE + HALF + cells, 8)

    sweeps(*band, [range(tiles + 1), range(tiles + 1, 2 * tiles + 2)], count, reach)
    for ring, top in ((0, 0), (tiles + 1, rows - HALF)):
        for tile in range(tiles):
            for field in range(5):
                live[field, tile, pl.ds(PAD + top, HALF), :] = band[0][field, ring + tile, pl.ds(EDGE, HALF), :]
    for hop, target in zip(later(blocks), outgoing):
        block = table[0, hop]
        emit(live, target, block * tall + outer_half(block, blocks), columns)


def collect_kernel(blocks, table, forcing, ice, live, *refs):
    early, (flux, out, own, sem) = refs[:-4], refs[-4:]
    rows, columns = ice.shape
    lat = lax.axis_index("lat")
    copies = []
    for hop, part in zip(soon(blocks), early):
        start = inner_half(table[1, hop], blocks)
        copies.append(pltpu.make_async_copy(part, out.at[lat ^ hop, :, pl.ds(start, HALF), :], sem.at[hop]))
        copies[-1].start()
    emit(live, own, table[0, 0] * (rows // blocks), columns)
    copies.append(pltpu.make_async_copy(own, out.at[lat], sem.at[0]))
    copies[-1].start()
    for tile in range(columns // LANES):
        for top in range(0, rows, 32):
            at = (pl.ds(top, 32), pl.ds(tile * LANES, LANES))
            span = pl.ds(PAD + top, 32)
            icy = DRAG * ice[at].astype(jnp.float32)
            flux[(0, *at)] = icy * (live[0, tile, span, :] - forcing[(2, *at)])
            flux[(1, *at)] = icy * (live[1, tile, span, :] - forcing[(3, *at)])
    for copy in copies:
        copy.wait()


def gather_kernel(blocks, table, *refs):
    late, (_, out, sem) = refs[:-3], refs[-3:]
    lat = lax.axis_index("lat")
    copies = []
    for hop, part in zip(later(blocks), late):
        start = outer_half(table[1, hop], blocks)
        copies.append(pltpu.make_async_copy(part, out.at[lat ^ hop, :, pl.ds(start, HALF), :], sem.at[hop - 1]))
        copies[-1].start()
    for copy in copies:
        copy.wait()


def spec(space=VMEM):
    return pl.BlockSpec(memory_space=space)


def params():
    return pltpu.CompilerParams(vmem_limit_bytes=16 << 20)


def cost(flops, data):
    return pl.CostEstimate(flops=flops, bytes_accessed=data, transcendentals=0)


def lon_swaps(a, b, lons):
    near = [(i, i ^ 1) for i in range(lons)]
    far = [(i, (i + 1 if i % 2 else i - 1) % lons) for i in range(lons)]
    return lax.ppermute(a, "lon", near), lax.ppermute(b, "lon", far)


def lat_swaps(a, b, lats, lons):
    near = [(i, i ^ 1) for i in range(lats)]
    far = []
    for i in range(lats):
        for j in range(lons):
            if i in (0, lats - 1):
                far.append((i * lons + j, i * lons + (j ^ 1)))
            else:
                far.append((i * lons + j, (i + 1 if i % 2 else i - 1) * lons + j))
    return lax.ppermute(a, "lat", near), lax.ppermute(b, ("lat", "lon"), far)


def per_device(ice_state, ocean_forcing, ice_strength, ice_mask, yield_mask, ice_route):
    f32 = jnp.float32
    count = yield_mask.shape[0]
    depth = 2 * count
    rows, columns = ice_strength.shape
    lats, lons = (lax.axis_size("lat"), lax.axis_size("lon"))
    tall = rows // lats
    inputs = (ice_route, ice_state, ocean_forcing, ice_strength, ice_mask, yield_mask)
    shape = jax.ShapeDtypeStruct
    lon_rim = shape((rows, LANES), f32)
    lat_rim = shape((depth * (FIELDS + 1), columns), f32)
    tiles = columns // LANES + 1

    def fields(tiles, rows):
        return [
            shape((5, tiles, rows, LANES), f32),
            shape((4, tiles, rows, LANES), f32),
            shape((tiles, rows, LANES), jnp.int32),
        ]

    inner, band = (fields(tiles - 1, rows + 2 * PAD), fields(2 * tiles, BAND))
    side = fields(1, rows + 2 * PAD)
    whole, half = (shape((5, tall, columns), f32), shape((5, HALF, columns), f32))
    lon_a, lon_b, lat_a, lat_b, route, *raw = pl.pallas_call(
        functools.partial(pack_kernel, depth),
        out_shape=[lon_rim] * 2 + [lat_rim] * 2 + [shape(x.shape, x.dtype) for x in inputs],
        in_specs=[spec(HBM)] * 6,
        out_specs=[spec()] * 10,
        scratch_shapes=[pltpu.SemaphoreType.DMA((3,))],
        compiler_params=params(),
        name="pack",
    )(*[pltpu.with_memory_space_constraint(x, HBM) for x in inputs])
    lon_a, lon_b = lon_swaps(lon_a, lon_b, lons)
    prepared = pl.pallas_call(
        functools.partial(prepare_kernel, depth),
        out_shape=inner + band + [shape((8, LANES), jnp.int32)] + side,
        in_specs=[spec()] * 6,
        out_specs=[spec()] * 10,
        compiler_params=params(),
        cost_estimate=cost(40 * rows * columns, 100 * rows * columns),
        name="prepare",
    )(route, *raw)
    table = prepared[6]
    live, _, _ = pl.pallas_call(
        functools.partial(inner_kernel, count),
        out_shape=inner,
        in_specs=[spec()] * 3,
        out_specs=[spec()] * 3,
        input_output_aliases={i: i for i in range(3)},
        compiler_params=params(),
        name="inner",
    )(*prepared[:3])
    lat_a, lat_b = pl.pallas_call(
        functools.partial(corner_kernel, depth),
        out_shape=[lat_rim] * 2,
        in_specs=[spec()] * 4 + [spec(pl.ANY)],
        out_specs=[spec()] * 2,
        input_output_aliases={2: 0, 3: 1},
        compiler_params=params(),
        name="corner",
    )(lon_a, lon_b, lat_a, lat_b, live)
    lat_a, lat_b = lat_swaps(lat_a, lat_b, lats, lons)

    def send(part, hop):
        return lax.ppermute(part, "lat", [(i, i ^ hop) for i in range(lats)])

    live, *rest = pl.pallas_call(
        functools.partial(sides_kernel, depth, count, lats),
        out_shape=inner[:1] + band + side + [half] * len(soon(lats)),
        in_specs=[spec()] * 10,
        out_specs=[spec()] * (7 + len(soon(lats))),
        input_output_aliases={3 + i: i for i in range(7)},
        compiler_params=params(),
        name="sides",
    )(table, lon_a, lon_b, live, *prepared[3:6], *prepared[7:])
    edges, early = (rest[:3], rest[6:])
    early = [send(part, hop) for hop, part in zip(soon(lats), early)]
    live, _, _, _, *late = pl.pallas_call(
        functools.partial(outer_kernel, depth, count, lats),
        out_shape=inner[:1] + band + [half] * len(later(lats)),
        in_specs=[spec()] * 7,
        out_specs=[spec()] * (4 + len(later(lats))),
        input_output_aliases={3 + i: i for i in range(4)},
        compiler_params=params(),
        name="outer",
    )(table, lat_b, lat_a, live, *edges)
    late = [send(part, hop) for hop, part in zip(later(lats), late)]
    result = shape((lats, *whole.shape), f32)
    flux, blocks = pl.pallas_call(
        functools.partial(collect_kernel, lats),
        out_shape=[shape((2, rows, columns), f32), result],
        in_specs=[spec()] * (4 + len(early)),
        out_specs=[spec(), spec(HBM)],
        scratch_shapes=[VMEM(whole.shape, f32), pltpu.SemaphoreType.DMA((lats,))],
        compiler_params=params(),
        name="collect",
    )(table, raw[1], raw[3], live, *early)
    blocks = pl.pallas_call(
        functools.partial(gather_kernel, lats),
        out_shape=result,
        in_specs=[spec()] * (1 + len(late)) + [spec(HBM)],
        out_specs=spec(HBM),
        scratch_shapes=[pltpu.SemaphoreType.DMA((len(late),))],
        input_output_aliases={1 + len(late): 0},
        compiler_params=params(),
        name="gather",
    )(table, *late, blocks)
    return flux, blocks


def solution(mesh):
    return jax.shard_map(
        per_device,
        mesh=mesh,
        in_specs=(
            P(None, "lat", "lon"),
            P(None, "lat", "lon"),
            P("lat", "lon"),
            P("lat", "lon"),
            P(None, "lat", "lon"),
            P(),
        ),
        out_specs=(P(None, "lat", "lon"), P("lat", None, None, "lon")),
        check_vma=False,
    )
```

```python
import functools
import jax
import jax.numpy as jnp
from jax import lax
from jax.experimental import pallas as pl
from jax.experimental.pallas import tpu as pltpu
from jax.sharding import PartitionSpec as P

DRAG = 0.5
SPIN = 0.15
DAMP = 0.8
LANES = 128
PAD = 8
BAND = 64
EDGE = 24
HALF = 16
FIELDS = 9
VMEM = pltpu.VMEM
HBM = pltpu.HBM


def lane_index(rows):
    return lax.broadcasted_iota(jnp.int32, (rows, LANES), 1)


def raw_fields(state, forcing, strength, ice, regimes, at):
    count = regimes.shape[0]
    s_one, s_two = (state[(2, *at)], state[(3, *at)])
    code = ice[at]
    for level in range(count):
        code = code + regimes[(level, *at)] * (2 << level)
    return [
        state[(0, *at)],
        state[(1, *at)],
        s_one + s_two,
        s_one - s_two,
        2.0 * state[(4, *at)],
        forcing[(0, *at)] + DRAG * forcing[(2, *at)],
        forcing[(1, *at)] + DRAG * forcing[(3, *at)],
        strength[at],
        code.astype(jnp.float32),
    ]


def rim_rows(depth):
    depths = [depth] * 2 + [depth - 1] * 3 + [depth - 2] * 2 + [depth - 1] * 2
    starts = [sum(depths[:field]) for field in range(FIELDS + 1)]
    return depths, starts


def both_axes():
    return (lax.axis_index("lat"), lax.axis_index("lon"))


def roll_to(value, shift):
    return value if shift % LANES == 0 else pltpu.roll(value, shift % LANES, 1)


def slotted(values, depth, start):
    lane = lane_index(values[0].shape[0])
    packed = roll_to(values[0], -start)
    for field in range(1, FIELDS):
        packed = jnp.where(lane >= depth * field, roll_to(values[field], depth * field - start), packed)
    return packed


def unslotted(west, east, depth):
    lane = lane_index(west.shape[0])
    fields = []
    for field in range(FIELDS):
        right = roll_to(east, -depth * field)
        left = roll_to(west, -depth * (field + 1))
        fields.append(jnp.where(lane < depth, right, jnp.where(lane >= LANES - depth, left, 0.0)))
    return fields


def pack_kernel(depth, *refs):
    sources, (lon_a, lon_b, lat_a, lat_b), held, sem = refs[:6], refs[6:10], refs[10:16], refs[16]
    rows, columns = held[3].shape
    waves = 2
    step = rows // waves
    copies = []
    for wave in range(waves):
        for source, target in zip(sources[1:], held[1:]):
            at = (slice(None),) * (len(source.shape) - 2) + (pl.ds(wave * step, step), slice(None))
            copies.append((wave, pltpu.make_async_copy(source.at[at], target.at[at], sem.at[wave])))
    copies.append((waves - 1, pltpu.make_async_copy(sources[0], held[0], sem.at[waves])))
    for _, copy in copies:
        copy.start()
    raw = held[1:]
    lat, lon = both_axes()
    lat_even = lax.rem(lat, 2) == 0
    lon_even = lax.rem(lon, 2) == 0
    for wave in range(waves):
        for index, copy in copies:
            if index == wave:
                copy.wait()
        for top in range(wave * step, (wave + 1) * step, 32):
            span = pl.ds(top, 32)
            first = slotted(raw_fields(*raw, (span, pl.ds(0, LANES))), depth, 0)
            last = slotted(raw_fields(*raw, (span, pl.ds(columns - LANES, LANES))), depth, LANES - depth)
            lon_a[span, :] = jnp.where(lon_even, last, first)
            lon_b[span, :] = jnp.where(lon_even, first, last)
    depths, starts = rim_rows(depth)
    for column in range(0, columns, LANES):
        here = pl.ds(column, LANES)
        first = raw_fields(*raw, (pl.ds(0, 16), here))
        last = raw_fields(*raw, (pl.ds(rows - 16, 16), here))
        for field, size in enumerate(depths):
            span = pl.ds(starts[field], size)
            one, two = (first[field][:size], last[field][16 - size :])
            lat_a[span, here] = jnp.where(lat_even, two, one)
            lat_b[span, here] = jnp.where(lat_even, one, two)


def corner_kernel(depth, lon_a, lon_b, lat_a, lat_b, after, out_a, out_b):
    rows = lon_a.shape[0]
    lat_even = lax.rem(lax.axis_index("lat"), 2) == 0
    span = pl.ds(rim_rows(depth)[1][-1], depth)
    for source, column in ((lon_a, 0), (lon_b, LANES)):
        first = source[pl.ds(0, 16), :][:depth]
        last = source[pl.ds(rows - 16, 16), :][16 - depth :]
        out_a[span, pl.ds(column, LANES)] = jnp.where(lat_even, last, first)
        out_b[span, pl.ds(column, LANES)] = jnp.where(lat_even, first, last)


def evolved(fields):
    u, v, a, b, t, fx, fy, strong, code = fields
    code = code.astype(jnp.int32)
    icy = (code & 1).astype(jnp.float32)
    kept = [u, v, icy * a, icy * b, icy * t]
    scales = [0.25 * icy * strong, DAMP * icy, (0.5 * DAMP) * icy * fx, (0.5 * DAMP) * icy * fy]
    return kept, scales, code


def place(live, coef, code_ref, tile, top, size, fields):
    span = pl.ds(top, size)
    kept, scales, code = evolved(fields)
    for field, value in enumerate(kept):
        live[field, tile, span, :] = value
    for field, value in enumerate(scales):
        coef[field, tile, span, :] = value
    code_ref[tile, span, :] = code


def prepare_kernel(depth, route, state, forcing, strength, ice, regimes, *refs):
    inner, band, table, side = refs[:3], refs[3:6], refs[6], refs[7:]
    lat = lax.axis_index("lat")
    line, lane = (lax.broadcasted_iota(jnp.int32, table.shape, axis) for axis in range(2))
    found = jnp.zeros(table.shape, jnp.int32)
    for hop in range(route.shape[0]):
        other = lat ^ hop
        for index, block in enumerate((block_for(route, lat, other), block_for(route, other, lat))):
            found = jnp.where((line == index) & (lane == hop), block, found)
    table[...] = found
    rows, columns = strength.shape
    tiles = columns // LANES

    def clear(refs, tile, top, size):
        span = pl.ds(top, size)
        zero = jnp.zeros((size, LANES), jnp.float32)
        for ref in refs[:2]:
            for field in range(ref.shape[0]):
                ref[field, tile, span, :] = zero
        refs[2][tile, span, :] = zero.astype(jnp.int32)

    for tile in range(tiles):
        clear(inner, tile, 0, PAD)
        clear(inner, tile, PAD + rows, PAD)
    for tile in range(tiles + 1):
        clear(band, tile, 0, EDGE)
        clear(band, tile, EDGE + 32, BAND - EDGE - 32)
        clear(band, tiles + 1 + tile, 0, 8)
        clear(band, tiles + 1 + tile, 40, BAND - 40)
    for field in range(5):
        for top in (0, PAD + rows):
            side[0][field, 0, pl.ds(top, PAD), :] = jnp.zeros((PAD, LANES), jnp.float32)
    lane = lane_index(32)
    own, middle = (2 * depth, LANES // 2)
    east = (lane >= middle - own) & (lane < middle)
    for top in range(0, rows, 32):
        ends = []
        for tile in range(tiles):
            at = (pl.ds(top, 32), pl.ds(tile * LANES, LANES))
            fields = raw_fields(state, forcing, strength, ice, regimes, at)
            place(*inner, tile, PAD + top, 32, fields)
            if top == 0:
                place(*band, tile, EDGE, 32, fields)
            if top == rows - 32:
                place(*band, tiles + 1 + tile, 8, 32, fields)
            if tile in (0, tiles - 1):
                ends.append(fields)
        both = zip(ends[0], ends[-1])
        joined = [jnp.where(lane < own, x, jnp.where(east, roll_to(y, middle), 0.0)) for x, y in both]
        place(*side, 0, PAD + top, 32, joined)


def sweeps(live, coef, code_ref, rings, count):
    size = 8
    lane = lane_index(size)
    first_lane = lane == 0
    last_lane = lane == LANES - 1

    def across(field, ring, top):
        parts = [row(field, tile, top) for tile in ring]
        back = [pltpu.roll(part, 1, 1) for part in parts]
        ahead = [pltpu.roll(part, LANES - 1, 1) for part in parts]
        wide = len(ring)
        return [
            jnp.where(last_lane, ahead[(i + 1) % wide], ahead[i])
            - jnp.where(first_lane, back[i - 1], back[i])
            for i in range(wide)
        ]

    def row(field, tile, top):
        return live[field, tile, pl.ds(top, size), :]

    def down(field, tile, top):
        return row(field, tile, top + 1) - row(field, tile, top - 1)

    for level in range(count):
        left = 2 * (count - level)
        for ring, reach in rings:
            for top in reach(left - 1):
                span = pl.ds(top, size)
                for tile, du_dx, dv_dx in zip(ring, across(0, ring, top), across(1, ring, top)):
                    dv_dy = down(1, tile, top)
                    du_dy = down(0, tile, top)
                    base = coef[0, tile, span, :]
                    weak = (code_ref[tile, span, :] & (2 << level)) != 0
                    scale = base * jnp.where(weak, 0.5, 1.5)
                    half = 0.5 * (du_dx + dv_dy)
                    live[2, tile, span, :] = 0.5 * row(2, tile, top) + (scale * (du_dx + half) - base)
                    live[3, tile, span, :] = 0.5 * row(3, tile, top) + (scale * (dv_dy + half) - base)
                    live[4, tile, span, :] = 0.5 * (row(4, tile, top) + scale * (du_dy + dv_dx))
        for ring, reach in rings:
            for top in reach(left - 2):
                span = pl.ds(top, size)
                for tile, da_dx, dt_dx in zip(ring, across(2, ring, top), across(4, ring, top)):
                    u, v = (row(0, tile, top), row(1, tile, top))
                    damp = coef[1, tile, span, :]
                    pull_x = 0.125 * (da_dx + down(4, tile, top))
                    pull_y = 0.125 * (down(3, tile, top) + dt_dx)
                    live[0, tile, span, :] = damp * (u + SPIN * v + pull_x) + coef[2, tile, span, :]
                    live[1, tile, span, :] = damp * (v - SPIN * u + pull_y) + coef[3, tile, span, :]


def rim_readers(depth, lats):
    lat, lon = both_axes()
    lat_even = lax.rem(lat, 2) == 0
    lon_even = lax.rem(lon, 2) == 0
    south = jnp.where(lat == lats - 1, 0.0, 1.0)
    north = jnp.where(lat == 0, 0.0, 1.0)

    def rim(a, b):
        return unslotted(jnp.where(lon_even, b, a), jnp.where(lon_even, a, b), depth)

    def from_north(a, b):
        return north * jnp.where(lat_even, b, a)

    def from_south(a, b):
        return south * jnp.where(lat_even, a, b)

    return rim, from_north, from_south


def block_for(route, band, target):
    return sum(jnp.where(route[band, j] == target, j, 0) for j in range(route.shape[1]))


def soon(blocks):
    return [*range(blocks - 1, 0, -1)]


def later(blocks):
    return [2, 1, *range(3, blocks)]


def inner_half(block, blocks):
    return pl.multiple_of(jnp.where(block == blocks - 1, 0, HALF), HALF)


def outer_half(block, blocks):
    return pl.multiple_of(jnp.where(block == blocks - 1, HALF, 0), HALF)


def finals(live, tile, span):
    u, v, a, b, t = (live[field, tile, span, :] for field in range(5))
    return (u, v, 0.5 * (a + b), 0.5 * (a - b), 0.5 * t)


def emit(live, target, start, columns):
    span = pl.ds(pl.multiple_of(PAD + start, 8), target.shape[1])
    for tile in range(columns // LANES):
        for field, value in enumerate(finals(live, tile, span)):
            target[field, :, pl.ds(tile * LANES, LANES)] = value


def inner_kernel(depth, count, *refs):
    inner = refs[3:]
    _, tiles, high, _ = inner[0].shape
    rows = high - 2 * PAD

    def reach(cells):
        return range(PAD + (depth - cells) // 8 * 8, PAD + rows - depth + cells, 8)

    sweeps(*inner, [(range(tiles), reach)], count)


def sides_kernel(depth, count, blocks, table, lon_a, lon_b, *refs):
    refs = refs[7:]
    live, band, side, outgoing = refs[0], refs[1:4], refs[4:7], refs[7:]
    rows = lon_a.shape[0]
    tiles = live.shape[1]
    columns = tiles * LANES
    rim, _, _ = rim_readers(depth, blocks)
    middle = LANES // 2
    lane = lane_index(32)
    west = lane >= LANES - depth
    east = (lane >= middle) & (lane < middle + depth)
    for top in range(0, rows, 32):
        span = pl.ds(top, 32)
        halo = rim(lon_a[span, :], lon_b[span, :])
        if top == 0:
            place(*band, tiles, EDGE, 32, halo)
        if top == rows - 32:
            place(*band, 2 * tiles + 1, 8, 32, halo)
        span = pl.ds(PAD + top, 32)
        kept, scales, code = evolved(halo)
        for ref, values in ((side[0], kept), (side[1], scales)):
            for field, value in enumerate(values):
                value = jnp.where(west, value, roll_to(value, middle))
                ref[field, 0, span, :] = jnp.where(west | east, value, ref[field, 0, span, :])
        code = jnp.where(west, code, roll_to(code, middle))
        side[2][0, span, :] = jnp.where(west | east, code, side[2][0, span, :])

    def reach(cells):
        return range(PAD + (depth - cells) // 8 * 8, PAD + rows - depth + cells, 8)

    sweeps(*side, [([0], reach)], count)
    lane = lane_index(8)
    for top in range(depth // 8 * 8, rows - depth // 8 * 8, 8):
        span = pl.ds(PAD + top, 8)
        for field in range(5):
            value = side[0][field, 0, span, :]
            for tile, fixed, inside in (
                (0, value, lane < depth),
                (tiles - 1, roll_to(value, middle), lane >= LANES - depth),
            ):
                live[field, tile, span, :] = jnp.where(inside, fixed, live[field, tile, span, :])
    for hop, target in zip(soon(blocks), outgoing):
        block = table[0, hop]
        emit(live, target, block * (rows // blocks) + inner_half(block, blocks), columns)


def outer_kernel(depth, count, blocks, table, lat_b, lat_a, *refs):
    refs = refs[4:]
    live, band, outgoing = refs[0], refs[1:4], refs[4:]
    rows, columns = (live.shape[2] - 2 * PAD, lat_a.shape[1])
    tiles = columns // LANES
    tall = rows // blocks
    rim, from_north, from_south = rim_readers(depth, blocks)
    depths, starts = rim_rows(depth)
    south = [pl.ds(start, depth) for start in starts]
    north = [pl.ds(start + size - depth, depth) for start, size in zip(starts, depths)]
    for ring, top, chosen, spans in ((0, EDGE - depth, from_north, north), (tiles + 1, 40, from_south, south[:-1])):
        for tile in range(tiles):
            here = pl.ds(tile * LANES, LANES)
            place(*band, ring + tile, top, depth, [chosen(lat_a[s, here], lat_b[s, here]) for s in spans])
        ends = south[-1]
        pair = [chosen(lat_a[ends, pl.ds(c, LANES)], lat_b[ends, pl.ds(c, LANES)]) for c in (0, LANES)]
        place(*band, ring + tiles, top, depth, rim(*pair))

    def reach_from(start):
        return lambda cells: range((start - cells) // 8 * 8, start + depth + cells, 8)

    below = 40 - depth
    rings = [(range(tiles + 1), reach_from(EDGE)), (range(tiles + 1, 2 * tiles + 2), reach_from(below))]
    sweeps(*band, rings, count)
    for ring, top, start in ((0, 0, EDGE), (tiles + 1, rows - depth, below)):
        for tile in range(tiles):
            for field in range(5):
                live[field, tile, pl.ds(PAD + top, depth), :] = band[0][field, ring + tile, pl.ds(start, depth), :]
    for hop, target in zip(later(blocks), outgoing):
        block = table[0, hop]
        emit(live, target, block * tall + outer_half(block, blocks), columns)


def collect_kernel(blocks, table, forcing, ice, live, *refs):
    early, (flux, out, own, sem) = refs[:-4], refs[-4:]
    rows, columns = ice.shape
    lat = lax.axis_index("lat")
    copies = []
    for hop, part in zip(soon(blocks), early):
        start = inner_half(table[1, hop], blocks)
        copies.append(pltpu.make_async_copy(part, out.at[lat ^ hop, :, pl.ds(start, HALF), :], sem.at[hop]))
        copies[-1].start()
    emit(live, own, table[0, 0] * (rows // blocks), columns)
    copies.append(pltpu.make_async_copy(own, out.at[lat], sem.at[0]))
    copies[-1].start()
    for tile in range(columns // LANES):
        for top in range(0, rows, 32):
            at = (pl.ds(top, 32), pl.ds(tile * LANES, LANES))
            span = pl.ds(PAD + top, 32)
            icy = DRAG * ice[at].astype(jnp.float32)
            flux[(0, *at)] = icy * (live[0, tile, span, :] - forcing[(2, *at)])
            flux[(1, *at)] = icy * (live[1, tile, span, :] - forcing[(3, *at)])
    for copy in copies:
        copy.wait()


def gather_kernel(blocks, table, *refs):
    late, (_, out, sem) = refs[:-3], refs[-3:]
    lat = lax.axis_index("lat")
    copies = []
    for hop, part in zip(later(blocks), late):
        start = outer_half(table[1, hop], blocks)
        copies.append(pltpu.make_async_copy(part, out.at[lat ^ hop, :, pl.ds(start, HALF), :], sem.at[hop - 1]))
        copies[-1].start()
    for copy in copies:
        copy.wait()


def spec(space=VMEM):
    return pl.BlockSpec(memory_space=space)


def params():
    return pltpu.CompilerParams(vmem_limit_bytes=16 << 20)


def cost(flops, data):
    return pl.CostEstimate(flops=flops, bytes_accessed=data, transcendentals=0)


def lon_swaps(a, b, lons):
    near = [(i, i ^ 1) for i in range(lons)]
    far = [(i, (i + 1 if i % 2 else i - 1) % lons) for i in range(lons)]
    return lax.ppermute(a, "lon", near), lax.ppermute(b, "lon", far)


def lat_swaps(a, b, lats, lons):
    near = [(i, i ^ 1) for i in range(lats)]
    far = []
    for i in range(lats):
        for j in range(lons):
            if i in (0, lats - 1):
                far.append((i * lons + j, i * lons + (j ^ 1)))
            else:
                far.append((i * lons + j, (i + 1 if i % 2 else i - 1) * lons + j))
    return lax.ppermute(a, "lat", near), lax.ppermute(b, ("lat", "lon"), far)


def per_device(ice_state, ocean_forcing, ice_strength, ice_mask, yield_mask, ice_route):
    f32 = jnp.float32
    count = yield_mask.shape[0]
    depth = 2 * count
    rows, columns = ice_strength.shape
    lats, lons = (lax.axis_size("lat"), lax.axis_size("lon"))
    tall = rows // lats
    inputs = (ice_route, ice_state, ocean_forcing, ice_strength, ice_mask, yield_mask)
    shape = jax.ShapeDtypeStruct
    lon_rim = shape((rows, LANES), f32)
    lat_rim = shape((rim_rows(depth)[1][-1] + depth, columns), f32)
    tiles = columns // LANES + 1

    def fields(tiles, rows):
        return [
            shape((5, tiles, rows, LANES), f32),
            shape((4, tiles, rows, LANES), f32),
            shape((tiles, rows, LANES), jnp.int32),
        ]

    inner, band = (fields(tiles - 1, rows + 2 * PAD), fields(2 * tiles, BAND))
    side = fields(1, rows + 2 * PAD)
    whole, half = (shape((5, tall, columns), f32), shape((5, HALF, columns), f32))
    lon_a, lon_b, lat_a, lat_b, route, *raw = pl.pallas_call(
        functools.partial(pack_kernel, depth),
        out_shape=[lon_rim] * 2 + [lat_rim] * 2 + [shape(x.shape, x.dtype) for x in inputs],
        in_specs=[spec(HBM)] * 6,
        out_specs=[spec()] * 10,
        scratch_shapes=[pltpu.SemaphoreType.DMA((3,))],
        compiler_params=params(),
        name="pack",
    )(*[pltpu.with_memory_space_constraint(x, HBM) for x in inputs])
    lon_a, lon_b = lon_swaps(lon_a, lon_b, lons)
    prepared = pl.pallas_call(
        functools.partial(prepare_kernel, depth),
        out_shape=inner + band + [shape((8, LANES), jnp.int32)] + side,
        in_specs=[spec()] * 6,
        out_specs=[spec()] * 10,
        compiler_params=params(),
        cost_estimate=cost(40 * rows * columns, 100 * rows * columns),
        name="prepare",
    )(route, *raw)
    table = prepared[6]
    live, _, _ = pl.pallas_call(
        functools.partial(inner_kernel, depth, count),
        out_shape=inner,
        in_specs=[spec()] * 3,
        out_specs=[spec()] * 3,
        input_output_aliases={i: i for i in range(3)},
        compiler_params=params(),
        name="inner",
    )(*prepared[:3])
    lat_a, lat_b = pl.pallas_call(
        functools.partial(corner_kernel, depth),
        out_shape=[lat_rim] * 2,
        in_specs=[spec()] * 4 + [spec(pl.ANY)],
        out_specs=[spec()] * 2,
        input_output_aliases={2: 0, 3: 1},
        compiler_params=params(),
        name="corner",
    )(lon_a, lon_b, lat_a, lat_b, live)
    lat_a, lat_b = lat_swaps(lat_a, lat_b, lats, lons)

    def send(part, hop):
        return lax.ppermute(part, "lat", [(i, i ^ hop) for i in range(lats)])

    live, *rest = pl.pallas_call(
        functools.partial(sides_kernel, depth, count, lats),
        out_shape=inner[:1] + band + side + [half] * len(soon(lats)),
        in_specs=[spec()] * 10,
        out_specs=[spec()] * (7 + len(soon(lats))),
        input_output_aliases={3 + i: i for i in range(7)},
        compiler_params=params(),
        name="sides",
    )(table, lon_a, lon_b, live, *prepared[3:6], *prepared[7:])
    edges, early = (rest[:3], rest[6:])
    early = [send(part, hop) for hop, part in zip(soon(lats), early)]
    live, _, _, _, *late = pl.pallas_call(
        functools.partial(outer_kernel, depth, count, lats),
        out_shape=inner[:1] + band + [half] * len(later(lats)),
        in_specs=[spec()] * 7,
        out_specs=[spec()] * (4 + len(later(lats))),
        input_output_aliases={3 + i: i for i in range(4)},
        compiler_params=params(),
        name="outer",
    )(table, lat_b, lat_a, live, *edges)
    late = [send(part, hop) for hop, part in zip(later(lats), late)]
    result = shape((lats, *whole.shape), f32)
    flux, blocks = pl.pallas_call(
        functools.partial(collect_kernel, lats),
        out_shape=[shape((2, rows, columns), f32), result],
        in_specs=[spec()] * (4 + len(early)),
        out_specs=[spec(), spec(HBM)],
        scratch_shapes=[VMEM(whole.shape, f32), pltpu.SemaphoreType.DMA((lats,))],
        compiler_params=params(),
        name="collect",
    )(table, raw[1], raw[3], live, *early)
    blocks = pl.pallas_call(
        functools.partial(gather_kernel, lats),
        out_shape=result,
        in_specs=[spec()] * (1 + len(late)) + [spec(HBM)],
        out_specs=spec(HBM),
        scratch_shapes=[pltpu.SemaphoreType.DMA((len(late),))],
        input_output_aliases={1 + len(late): 0},
        compiler_params=params(),
        name="gather",
    )(table, *late, blocks)
    return flux, blocks


def solution(mesh):
    return jax.shard_map(
        per_device,
        mesh=mesh,
        in_specs=(
            P(None, "lat", "lon"),
            P(None, "lat", "lon"),
            P("lat", "lon"),
            P("lat", "lon"),
            P(None, "lat", "lon"),
            P(),
        ),
        out_specs=(P(None, "lat", "lon"), P("lat", None, None, "lon")),
        check_vma=False,
    )
```

```python
import functools
import jax
import jax.numpy as jnp
from jax import lax
from jax.experimental import pallas as pl
from jax.experimental.pallas import tpu as pltpu
from jax.sharding import PartitionSpec as P

DRAG = 0.5
SPIN = 0.15
DAMP = 0.8
LANES = 128
PAD = 8
BAND = 64
EDGE = 24
HALF = 16
FIELDS = 9
VMEM = pltpu.VMEM
HBM = pltpu.HBM


def lane_index(rows):
    return lax.broadcasted_iota(jnp.int32, (rows, LANES), 1)


def raw_fields(state, forcing, strength, ice, regimes, at):
    count = regimes.shape[0]
    s_one, s_two = (state[(2, *at)], state[(3, *at)])
    code = ice[at]
    for level in range(count):
        code = code + regimes[(level, *at)] * (2 << level)
    return [
        state[(0, *at)],
        state[(1, *at)],
        s_one + s_two,
        s_one - s_two,
        2.0 * state[(4, *at)],
        forcing[(0, *at)] + DRAG * forcing[(2, *at)],
        forcing[(1, *at)] + DRAG * forcing[(3, *at)],
        strength[at],
        code.astype(jnp.float32),
    ]


def both_axes():
    return (lax.axis_index("lat"), lax.axis_index("lon"))


def roll_to(value, shift):
    return value if shift % LANES == 0 else pltpu.roll(value, shift % LANES, 1)


def slotted(values, depth, start):
    lane = lane_index(values[0].shape[0])
    packed = roll_to(values[0], -start)
    for field in range(1, FIELDS):
        packed = jnp.where(lane >= depth * field, roll_to(values[field], depth * field - start), packed)
    return packed


def unslotted(west, east, depth):
    lane = lane_index(west.shape[0])
    fields = []
    for field in range(FIELDS):
        right = roll_to(east, -depth * field)
        left = roll_to(west, -depth * (field + 1))
        fields.append(jnp.where(lane < depth, right, jnp.where(lane >= LANES - depth, left, 0.0)))
    return fields


def pack_kernel(depth, *refs):
    sources, (lon_a, lon_b, lat_a, lat_b), held, sem = refs[:6], refs[6:10], refs[10:16], refs[16]
    rows, columns = held[3].shape
    waves = 2
    step = rows // waves
    copies = []
    for wave in range(waves):
        for source, target in zip(sources[1:], held[1:]):
            at = (slice(None),) * (len(source.shape) - 2) + (pl.ds(wave * step, step), slice(None))
            copies.append((wave, pltpu.make_async_copy(source.at[at], target.at[at], sem.at[wave])))
    copies.append((waves - 1, pltpu.make_async_copy(sources[0], held[0], sem.at[waves])))
    for _, copy in copies:
        copy.start()
    raw = held[1:]
    lat, lon = both_axes()
    lat_even = lax.rem(lat, 2) == 0
    lon_even = lax.rem(lon, 2) == 0
    for wave in range(waves):
        for index, copy in copies:
            if index == wave:
                copy.wait()
        for top in range(wave * step, (wave + 1) * step, 32):
            span = pl.ds(top, 32)
            first = slotted(raw_fields(*raw, (span, pl.ds(0, LANES))), depth, 0)
            last = slotted(raw_fields(*raw, (span, pl.ds(columns - LANES, LANES))), depth, LANES - depth)
            lon_a[span, :] = jnp.where(lon_even, last, first)
            lon_b[span, :] = jnp.where(lon_even, first, last)
    for column in range(0, columns, LANES):
        here = pl.ds(column, LANES)
        first = raw_fields(*raw, (pl.ds(0, 16), here))
        last = raw_fields(*raw, (pl.ds(rows - 16, 16), here))
        for field in range(FIELDS):
            span = pl.ds(depth * field, depth)
            one, two = (first[field][:depth], last[field][16 - depth :])
            lat_a[span, here] = jnp.where(lat_even, two, one)
            lat_b[span, here] = jnp.where(lat_even, one, two)


def corner_kernel(depth, lon_a, lon_b, lat_a, lat_b, after, out_a, out_b):
    rows = lon_a.shape[0]
    lat_even = lax.rem(lax.axis_index("lat"), 2) == 0
    span = pl.ds(depth * FIELDS, depth)
    for source, column in ((lon_a, 0), (lon_b, LANES)):
        first = source[pl.ds(0, 16), :][:depth]
        last = source[pl.ds(rows - 16, 16), :][16 - depth :]
        out_a[span, pl.ds(column, LANES)] = jnp.where(lat_even, last, first)
        out_b[span, pl.ds(column, LANES)] = jnp.where(lat_even, first, last)


def evolved(fields):
    u, v, a, b, t, fx, fy, strong, code = fields
    code = code.astype(jnp.int32)
    icy = (code & 1).astype(jnp.float32)
    kept = [u, v, icy * a, icy * b, icy * t]
    scales = [0.25 * icy * strong, DAMP * icy, (0.5 * DAMP) * icy * fx, (0.5 * DAMP) * icy * fy]
    return kept, scales, code


def place(live, coef, code_ref, tile, top, size, fields):
    span = pl.ds(top, size)
    kept, scales, code = evolved(fields)
    for field, value in enumerate(kept):
        live[field, tile, span, :] = value
    for field, value in enumerate(scales):
        coef[field, tile, span, :] = value
    code_ref[tile, span, :] = code


def prepare_kernel(depth, route, state, forcing, strength, ice, regimes, *refs):
    inner, band, table, side = refs[:3], refs[3:6], refs[6], refs[7:]
    lat = lax.axis_index("lat")
    line, lane = (lax.broadcasted_iota(jnp.int32, table.shape, axis) for axis in range(2))
    found = jnp.zeros(table.shape, jnp.int32)
    for hop in range(route.shape[0]):
        other = lat ^ hop
        for index, block in enumerate((block_for(route, lat, other), block_for(route, other, lat))):
            found = jnp.where((line == index) & (lane == hop), block, found)
    table[...] = found
    rows, columns = strength.shape
    tiles = columns // LANES

    def clear(refs, tile, top, size):
        span = pl.ds(top, size)
        zero = jnp.zeros((size, LANES), jnp.float32)
        for ref in refs[:2]:
            for field in range(ref.shape[0]):
                ref[field, tile, span, :] = zero
        refs[2][tile, span, :] = zero.astype(jnp.int32)

    for tile in range(tiles):
        clear(inner, tile, 0, PAD)
        clear(inner, tile, PAD + rows, PAD)
    for tile in range(tiles + 1):
        clear(band, tile, 0, EDGE)
        clear(band, tile, EDGE + 32, BAND - EDGE - 32)
        clear(band, tiles + 1 + tile, 0, 8)
        clear(band, tiles + 1 + tile, 40, BAND - 40)
    for field in range(5):
        for top in (0, PAD + rows):
            side[0][field, 0, pl.ds(top, PAD), :] = jnp.zeros((PAD, LANES), jnp.float32)
    lane = lane_index(32)
    own, middle = (2 * depth, LANES // 2)
    east = (lane >= middle - own) & (lane < middle)
    for top in range(0, rows, 32):
        ends = []
        for tile in range(tiles):
            at = (pl.ds(top, 32), pl.ds(tile * LANES, LANES))
            fields = raw_fields(state, forcing, strength, ice, regimes, at)
            place(*inner, tile, PAD + top, 32, fields)
            if top == 0:
                place(*band, tile, EDGE, 32, fields)
            if top == rows - 32:
                place(*band, tiles + 1 + tile, 8, 32, fields)
            if tile in (0, tiles - 1):
                ends.append(fields)
        both = zip(ends[0], ends[-1])
        joined = [jnp.where(lane < own, x, jnp.where(east, roll_to(y, middle), 0.0)) for x, y in both]
        place(*side, 0, PAD + top, 32, joined)


def sweeps(live, coef, code_ref, rings, count, reach):
    size = 8
    lane = lane_index(size)
    first_lane = lane == 0
    last_lane = lane == LANES - 1

    def across(field, ring, top):
        parts = [row(field, tile, top) for tile in ring]
        back = [pltpu.roll(part, 1, 1) for part in parts]
        ahead = [pltpu.roll(part, LANES - 1, 1) for part in parts]
        wide = len(ring)
        return [
            jnp.where(last_lane, ahead[(i + 1) % wide], ahead[i])
            - jnp.where(first_lane, back[i - 1], back[i])
            for i in range(wide)
        ]

    def row(field, tile, top):
        return live[field, tile, pl.ds(top, size), :]

    def down(field, tile, top):
        return row(field, tile, top + 1) - row(field, tile, top - 1)

    for level in range(count):
        left = 2 * (count - level)
        for ring in rings:
            for top in reach(left - 1):
                span = pl.ds(top, size)
                for tile, du_dx, dv_dx in zip(ring, across(0, ring, top), across(1, ring, top)):
                    dv_dy = down(1, tile, top)
                    du_dy = down(0, tile, top)
                    base = coef[0, tile, span, :]
                    weak = (code_ref[tile, span, :] & (2 << level)) != 0
                    scale = base * jnp.where(weak, 0.5, 1.5)
                    half = 0.5 * (du_dx + dv_dy)
                    live[2, tile, span, :] = 0.5 * row(2, tile, top) + (scale * (du_dx + half) - base)
                    live[3, tile, span, :] = 0.5 * row(3, tile, top) + (scale * (dv_dy + half) - base)
                    live[4, tile, span, :] = 0.5 * (row(4, tile, top) + scale * (du_dy + dv_dx))
        for ring in rings:
            for top in reach(left - 2):
                span = pl.ds(top, size)
                for tile, da_dx, dt_dx in zip(ring, across(2, ring, top), across(4, ring, top)):
                    u, v = (row(0, tile, top), row(1, tile, top))
                    damp = coef[1, tile, span, :]
                    pull_x = 0.125 * (da_dx + down(4, tile, top))
                    pull_y = 0.125 * (down(3, tile, top) + dt_dx)
                    live[0, tile, span, :] = damp * (u + SPIN * v + pull_x) + coef[2, tile, span, :]
                    live[1, tile, span, :] = damp * (v - SPIN * u + pull_y) + coef[3, tile, span, :]


def rim_readers(depth, lats):
    lat, lon = both_axes()
    lat_even = lax.rem(lat, 2) == 0
    lon_even = lax.rem(lon, 2) == 0
    south = jnp.where(lat == lats - 1, 0.0, 1.0)
    north = jnp.where(lat == 0, 0.0, 1.0)

    def rim(a, b):
        return unslotted(jnp.where(lon_even, b, a), jnp.where(lon_even, a, b), depth)

    def from_north(a, b):
        return north * jnp.where(lat_even, b, a)

    def from_south(a, b):
        return south * jnp.where(lat_even, a, b)

    return rim, from_north, from_south


def block_for(route, band, target):
    return sum(jnp.where(route[band, j] == target, j, 0) for j in range(route.shape[1]))


def soon(blocks):
    return [*range(blocks - 1, 0, -1)]


def later(blocks):
    return [2, 1, *range(3, blocks)]


def inner_half(block, blocks):
    return pl.multiple_of(jnp.where(block == blocks - 1, 0, HALF), HALF)


def outer_half(block, blocks):
    return pl.multiple_of(jnp.where(block == blocks - 1, HALF, 0), HALF)


def finals(live, tile, span):
    u, v, a, b, t = (live[field, tile, span, :] for field in range(5))
    return (u, v, 0.5 * (a + b), 0.5 * (a - b), 0.5 * t)


def emit(live, target, start, columns):
    span = pl.ds(pl.multiple_of(PAD + start, 8), target.shape[1])
    for tile in range(columns // LANES):
        for field, value in enumerate(finals(live, tile, span)):
            target[field, :, pl.ds(tile * LANES, LANES)] = value


def inner_kernel(depth, count, *refs):
    prepare_kernel(depth, *refs)
    inner = refs[6:9]
    _, tiles, high, _ = inner[0].shape
    rows = high - 2 * PAD

    def reach(cells):
        return range(PAD + (HALF - cells) // 8 * 8, PAD + rows - HALF + cells, 8)

    sweeps(*inner, [range(tiles)], count, reach)


def sides_kernel(depth, count, blocks, table, lon_a, lon_b, *refs):
    refs = refs[7:]
    live, band, side, outgoing = refs[0], refs[1:4], refs[4:7], refs[7:]
    rows = lon_a.shape[0]
    tiles = live.shape[1]
    columns = tiles * LANES
    rim, _, _ = rim_readers(depth, blocks)
    middle = LANES // 2
    lane = lane_index(32)
    west = lane >= LANES - depth
    east = (lane >= middle) & (lane < middle + depth)
    for top in range(0, rows, 32):
        span = pl.ds(top, 32)
        halo = rim(lon_a[span, :], lon_b[span, :])
        if top == 0:
            place(*band, tiles, EDGE, 32, halo)
        if top == rows - 32:
            place(*band, 2 * tiles + 1, 8, 32, halo)
        span = pl.ds(PAD + top, 32)
        kept, scales, code = evolved(halo)
        for ref, values in ((side[0], kept), (side[1], scales)):
            for field, value in enumerate(values):
                value = jnp.where(west, value, roll_to(value, middle))
                ref[field, 0, span, :] = jnp.where(west | east, value, ref[field, 0, span, :])
        code = jnp.where(west, code, roll_to(code, middle))
        side[2][0, span, :] = jnp.where(west | east, code, side[2][0, span, :])

    def reach(cells):
        return range(PAD + (HALF - cells) // 8 * 8, PAD + rows - HALF + cells, 8)

    sweeps(*side, [[0]], count, reach)
    lane = lane_index(16)
    for top in range(HALF, rows - HALF, 16):
        span = pl.ds(PAD + top, 16)
        for field in range(5):
            value = side[0][field, 0, span, :]
            for tile, fixed, inside in (
                (0, value, lane < depth),
                (tiles - 1, roll_to(value, middle), lane >= LANES - depth),
            ):
                live[field, tile, span, :] = jnp.where(inside, fixed, live[field, tile, span, :])
    for hop, target in zip(soon(blocks), outgoing):
        block = table[0, hop]
        emit(live, target, block * (rows // blocks) + inner_half(block, blocks), columns)


def outer_kernel(depth, count, blocks, table, lat_b, lat_a, *refs):
    refs = refs[4:]
    live, band, outgoing = refs[0], refs[1:4], refs[4:]
    rows, columns = (live.shape[2] - 2 * PAD, lat_a.shape[1])
    tiles = columns // LANES
    tall = rows // blocks
    rim, from_north, from_south = rim_readers(depth, blocks)
    spans = [pl.ds(depth * f, depth) for f in range(FIELDS + 1)]
    for ring, top, chosen in ((0, EDGE - depth, from_north), (tiles + 1, 40, from_south)):
        for tile in range(tiles):
            here = pl.ds(tile * LANES, LANES)
            place(*band, ring + tile, top, depth, [chosen(lat_a[s, here], lat_b[s, here]) for s in spans[:-1]])
        pair = [chosen(lat_a[spans[-1], pl.ds(c, LANES)], lat_b[spans[-1], pl.ds(c, LANES)]) for c in (0, LANES)]
        place(*band, ring + tiles, top, depth, rim(*pair))

    def reach(cells):
        return range((EDGE - cells) // 8 * 8, EDGE + HALF + cells, 8)

    sweeps(*band, [range(tiles + 1), range(tiles + 1, 2 * tiles + 2)], count, reach)
    for ring, top in ((0, 0), (tiles + 1, rows - HALF)):
        for tile in range(tiles):
            for field in range(5):
                live[field, tile, pl.ds(PAD + top, HALF), :] = band[0][field, ring + tile, pl.ds(EDGE, HALF), :]
    for hop, target in zip(later(blocks), outgoing):
        block = table[0, hop]
        emit(live, target, block * tall + outer_half(block, blocks), columns)


def collect_kernel(blocks, table, forcing, ice, live, *refs):
    early, (flux, out, own, sem) = refs[:-4], refs[-4:]
    rows, columns = ice.shape
    lat = lax.axis_index("lat")
    copies = []
    for hop, part in zip(soon(blocks), early):
        start = inner_half(table[1, hop], blocks)
        copies.append(pltpu.make_async_copy(part, out.at[lat ^ hop, :, pl.ds(start, HALF), :], sem.at[hop]))
        copies[-1].start()
    emit(live, own, table[0, 0] * (rows // blocks), columns)
    copies.append(pltpu.make_async_copy(own, out.at[lat], sem.at[0]))
    copies[-1].start()
    for tile in range(columns // LANES):
        for top in range(0, rows, 32):
            at = (pl.ds(top, 32), pl.ds(tile * LANES, LANES))
            span = pl.ds(PAD + top, 32)
            icy = DRAG * ice[at].astype(jnp.float32)
            flux[(0, *at)] = icy * (live[0, tile, span, :] - forcing[(2, *at)])
            flux[(1, *at)] = icy * (live[1, tile, span, :] - forcing[(3, *at)])
    for copy in copies:
        copy.wait()


def gather_kernel(blocks, table, *refs):
    late, (_, out, sem) = refs[:-3], refs[-3:]
    lat = lax.axis_index("lat")
    copies = []
    for hop, part in zip(later(blocks), late):
        start = outer_half(table[1, hop], blocks)
        copies.append(pltpu.make_async_copy(part, out.at[lat ^ hop, :, pl.ds(start, HALF), :], sem.at[hop - 1]))
        copies[-1].start()
    for copy in copies:
        copy.wait()


def spec(space=VMEM):
    return pl.BlockSpec(memory_space=space)


def params():
    return pltpu.CompilerParams(vmem_limit_bytes=16 << 20)


def cost(flops, data):
    return pl.CostEstimate(flops=flops, bytes_accessed=data, transcendentals=0)


def lon_swaps(a, b, lons):
    near = [(i, i ^ 1) for i in range(lons)]
    far = [(i, (i + 1 if i % 2 else i - 1) % lons) for i in range(lons)]
    return lax.ppermute(a, "lon", near), lax.ppermute(b, "lon", far)


def lat_swaps(a, b, lats, lons):
    near = [(i, i ^ 1) for i in range(lats)]
    far = []
    for i in range(lats):
        for j in range(lons):
            if i in (0, lats - 1):
                far.append((i * lons + j, i * lons + (j ^ 1)))
            else:
                far.append((i * lons + j, (i + 1 if i % 2 else i - 1) * lons + j))
    return lax.ppermute(a, "lat", near), lax.ppermute(b, ("lat", "lon"), far)


def per_device(ice_state, ocean_forcing, ice_strength, ice_mask, yield_mask, ice_route):
    f32 = jnp.float32
    count = yield_mask.shape[0]
    depth = 2 * count
    rows, columns = ice_strength.shape
    lats, lons = (lax.axis_size("lat"), lax.axis_size("lon"))
    tall = rows // lats
    inputs = (ice_route, ice_state, ocean_forcing, ice_strength, ice_mask, yield_mask)
    shape = jax.ShapeDtypeStruct
    lon_rim = shape((rows, LANES), f32)
    lat_rim = shape((depth * (FIELDS + 1), columns), f32)
    tiles = columns // LANES + 1

    def fields(tiles, rows):
        return [
            shape((5, tiles, rows, LANES), f32),
            shape((4, tiles, rows, LANES), f32),
            shape((tiles, rows, LANES), jnp.int32),
        ]

    inner, band = (fields(tiles - 1, rows + 2 * PAD), fields(2 * tiles, BAND))
    side = fields(1, rows + 2 * PAD)
    whole, half = (shape((5, tall, columns), f32), shape((5, HALF, columns), f32))
    lon_a, lon_b, lat_a, lat_b, route, *raw = pl.pallas_call(
        functools.partial(pack_kernel, depth),
        out_shape=[lon_rim] * 2 + [lat_rim] * 2 + [shape(x.shape, x.dtype) for x in inputs],
        in_specs=[spec(HBM)] * 6,
        out_specs=[spec()] * 10,
        scratch_shapes=[pltpu.SemaphoreType.DMA((3,))],
        compiler_params=params(),
        name="pack",
    )(*[pltpu.with_memory_space_constraint(x, HBM) for x in inputs])
    lon_a, lon_b = lon_swaps(lon_a, lon_b, lons)
    prepared = pl.pallas_call(
        functools.partial(inner_kernel, depth, count),
        out_shape=inner + band + [shape((8, LANES), jnp.int32)] + side,
        in_specs=[spec()] * 6,
        out_specs=[spec()] * 10,
        compiler_params=params(),
        cost_estimate=cost(40 * rows * columns, 100 * rows * columns),
        name="inner",
    )(route, *raw)
    table = prepared[6]
    live = prepared[0]
    lat_a, lat_b = pl.pallas_call(
        functools.partial(corner_kernel, depth),
        out_shape=[lat_rim] * 2,
        in_specs=[spec()] * 4 + [spec(pl.ANY)],
        out_specs=[spec()] * 2,
        input_output_aliases={2: 0, 3: 1},
        compiler_params=params(),
        name="corner",
    )(lon_a, lon_b, lat_a, lat_b, live)
    lat_a, lat_b = lat_swaps(lat_a, lat_b, lats, lons)

    def send(part, hop):
        return lax.ppermute(part, "lat", [(i, i ^ hop) for i in range(lats)])

    live, *rest = pl.pallas_call(
        functools.partial(sides_kernel, depth, count, lats),
        out_shape=inner[:1] + band + side + [half] * len(soon(lats)),
        in_specs=[spec()] * 10,
        out_specs=[spec()] * (7 + len(soon(lats))),
        input_output_aliases={3 + i: i for i in range(7)},
        compiler_params=params(),
        name="sides",
    )(table, lon_a, lon_b, live, *prepared[3:6], *prepared[7:])
    edges, early = (rest[:3], rest[6:])
    early = [send(part, hop) for hop, part in zip(soon(lats), early)]
    live, _, _, _, *late = pl.pallas_call(
        functools.partial(outer_kernel, depth, count, lats),
        out_shape=inner[:1] + band + [half] * len(later(lats)),
        in_specs=[spec()] * 7,
        out_specs=[spec()] * (4 + len(later(lats))),
        input_output_aliases={3 + i: i for i in range(4)},
        compiler_params=params(),
        name="outer",
    )(table, lat_b, lat_a, live, *edges)
    late = [send(part, hop) for hop, part in zip(later(lats), late)]
    result = shape((lats, *whole.shape), f32)
    flux, blocks = pl.pallas_call(
        functools.partial(collect_kernel, lats),
        out_shape=[shape((2, rows, columns), f32), result],
        in_specs=[spec()] * (4 + len(early)),
        out_specs=[spec(), spec(HBM)],
        scratch_shapes=[VMEM(whole.shape, f32), pltpu.SemaphoreType.DMA((lats,))],
        compiler_params=params(),
        name="collect",
    )(table, raw[1], raw[3], live, *early)
    blocks = pl.pallas_call(
        functools.partial(gather_kernel, lats),
        out_shape=result,
        in_specs=[spec()] * (1 + len(late)) + [spec(HBM)],
        out_specs=spec(HBM),
        scratch_shapes=[pltpu.SemaphoreType.DMA((len(late),))],
        input_output_aliases={1 + len(late): 0},
        compiler_params=params(),
        name="gather",
    )(table, *late, blocks)
    return flux, blocks


def solution(mesh):
    return jax.shard_map(
        per_device,
        mesh=mesh,
        in_specs=(
            P(None, "lat", "lon"),
            P(None, "lat", "lon"),
            P("lat", "lon"),
            P("lat", "lon"),
            P(None, "lat", "lon"),
            P(),
        ),
        out_specs=(P(None, "lat", "lon"), P("lat", None, None, "lon")),
        check_vma=False,
    )
```
